32 devices in a mesh: rows: 16 (over z, x, core), rep: 2 (over y).
Axes of the slice: x: 2, y: 2, z: 4, core: 2. Of those that a mesh axis runs over, the one named last changes fastest.
Arguments:
- features: bfloat16 [12288, 256], P('rows'), may hold values from -6 to 6
- tiles: bfloat16 [96, 12, 128, 128], P('rows', 'rep'), may hold values from -0.21875 to 0.21875
- columns: int32 [96, 12], P('rows', 'rep'), may hold values from 0 to 95, as said below
- live: int32 [96, 2], P('rows', 'rep'), may hold values from 1 to 6, as said below
- weight: bfloat16 [256, 256], replicated, may hold values from -0.375 to 0.375
- bias: float32 [256], replicated, may hold values from -3 to 3
- cotangent: bfloat16 [12288, 256], P('rows'), may hold values from -6 to 6
Outputs:
- activations: bfloat16 [12288, 256], P('rows')
- feature_grad: bfloat16 [12288, 256], P('rows')
- weight_grad: float32 [256, 256], replicated
- bias_grad: float32 [256], replicated
The draws below stay inside these ranges and needn't reach their ends.
Inputs may be any that keep to these rules, and one draw needn't show every extreme that they name: `columns`: the 12 slots of row block g name, in some order, each of the blocks s to s + 2 * 6 - 1 once, where s = g - 6 clipped to 0 .. 84. `live`: 1 to 6 live slots in each half of a row block's slots; some row block in every draw has all 6 live in its first half.
All inputs are finite; a program needn't handle non-finite values.
Results may differ from the reference program's by a relative error of at most 0.0061.
Values may be sent and summed in bfloat16 or wider, within the bound.
A program may use at most 64 MiB of HBM per device.

```python
import math
import jax
import jax.numpy as jnp
from jax import lax

F = 256
TILE = 128
NB = 6
SLOTS = 6
NBLOCKS = 96
NODES = 12288
N_ROWS = 16


def draw_columns(key, part):
    block_ids = jnp.arange(NBLOCKS, dtype=jnp.int32)
    window_start = jnp.clip(block_ids - NB, 0, NBLOCKS - 2 * NB)
    row_keys = jax.random.split(key, NBLOCKS)
    orders = jax.vmap(lambda one_key: jax.random.permutation(one_key, 2 * NB))(row_keys)
    return (window_start[:, None] + orders.astype(jnp.int32)).astype(jnp.int32)


def draw_live(key, part):
    counts = jax.random.randint(key, (NBLOCKS, 2), 1, SLOTS + 1, dtype=jnp.int32)
    block_ids = jnp.arange(NBLOCKS, dtype=jnp.int32)
    first_half = jnp.where(block_ids % 4 == 0, SLOTS, counts[:, 0])
    return counts.at[:, 0].set(first_half).astype(jnp.int32)


def block_levels(stream_key, shape, cuts, smallest, high):
    loudness, own = 1.0, jax.random.fold_in(stream_key, 6)
    for position, shards_of in cuts:
        draws = jnp.exp(jax.random.uniform(jax.random.fold_in(own, position), (shards_of,), jnp.float32, smallest / len(cuts), high / len(cuts)))
        loudness = loudness * jnp.repeat(draws, shape[position] // shards_of).reshape([-1 if axis == position else 1 for axis in range(len(shape))])
    return loudness


def bell_draw(stream_key, extent, scale, most, pieces=(), kind=jnp.bfloat16):
    array = jax.random.normal(stream_key, extent, jnp.float32) * scale
    if len(pieces) > 0:
        array = block_levels(stream_key, extent, pieces, -0.22, 0.18) * array
    return jnp.clip(array, min=-most, max=most).astype(kind)


def setup_inputs(seed: int = 0) -> dict:
    arg_keys = jax.random.split(jax.random.key(seed), 8)
    features = bell_draw(arg_keys[0], (NODES, F), 1.0, 6.0, ((0, 16),))
    tiles = bell_draw(arg_keys[1], (NBLOCKS, 2 * SLOTS, TILE, TILE), (TILE * SLOTS) ** -0.5, 0.21875, ((0, 16), (1, 2)))
    columns = draw_columns(jax.random.fold_in(arg_keys[7], 71), 0)
    live = draw_live(jax.random.fold_in(arg_keys[7], 71), 0)
    weight = bell_draw(arg_keys[4], (F, F), F ** -0.5, 0.375)
    bias = bell_draw(arg_keys[5], (F,), 0.5, 3.0, (), jnp.float32)
    cotangent = bell_draw(arg_keys[6], (NODES, F), 1.0, 6.0, ((0, 16),))
    return dict(features=features, tiles=tiles, columns=columns, live=live, weight=weight, bias=bias, cotangent=cotangent)


def reference(features, tiles, columns, live, weight, bias, cotangent):
    node_count = features.shape[0]
    block_count = columns.shape[0]
    tile_size = tiles.shape[2]
    slot_total = columns.shape[1]
    slot_ids = jnp.arange(slot_total, dtype=jnp.int32)
    half_index = slot_ids // SLOTS
    within = slot_ids % SLOTS
    live_mask = within[None, :] < live[:, half_index]
    feat_blocks = features.reshape(block_count, tile_size, F)

    def aggregate_group(group):
        start = (group * NB).astype(jnp.int32)
        tile_part = lax.dynamic_slice_in_dim(tiles, start, NB, 0)
        col_part = lax.dynamic_slice_in_dim(columns, start, NB, 0)
        mask_part = lax.dynamic_slice_in_dim(live_mask, start, NB, 0)
        gathered = feat_blocks[col_part] * mask_part[:, :, None, None].astype(jnp.bfloat16)
        return jnp.einsum('bkij,bkjf->bif', tile_part.astype(jnp.float32), gathered.astype(jnp.float32))
    aggregate = lax.map(aggregate_group, jnp.arange(N_ROWS, dtype=jnp.int32))
    aggregate = aggregate.reshape(node_count, F).astype(jnp.bfloat16)
    pre_act = jnp.dot(aggregate, weight, preferred_element_type=jnp.float32) + bias
    activations = jax.nn.silu(pre_act).astype(jnp.bfloat16)
    sigmoid_pre = jax.nn.sigmoid(pre_act)
    pre_grad = (cotangent.astype(jnp.float32) * sigmoid_pre * (1.0 + pre_act * (1.0 - sigmoid_pre))).astype(jnp.bfloat16)
    agg_grad = jnp.dot(pre_grad, weight.T, preferred_element_type=jnp.float32).astype(jnp.bfloat16)
    grad_blocks = agg_grad.reshape(block_count, tile_size, F)

    def spread_group(buffer, group):
        start = (group * NB).astype(jnp.int32)
        tile_part = lax.dynamic_slice_in_dim(tiles, start, NB, 0)
        col_part = lax.dynamic_slice_in_dim(columns, start, NB, 0)
        mask_part = lax.dynamic_slice_in_dim(live_mask, start, NB, 0)
        grad_part = lax.dynamic_slice_in_dim(grad_blocks, start, NB, 0)
        contrib = jnp.einsum('bkij,bif->bkjf', tile_part.astype(jnp.float32), grad_part.astype(jnp.float32))
        contrib = contrib * mask_part[:, :, None, None].astype(jnp.float32)
        buffer = buffer.at[col_part.reshape(-1)].add(contrib.reshape(-1, tile_size, F))
        return (buffer, None)
    buffer = jnp.zeros((block_count, tile_size, F), jnp.float32)
    buffer, unused = lax.scan(spread_group, buffer, jnp.arange(N_ROWS, dtype=jnp.int32))
    feature_grad = buffer.reshape(node_count, F).astype(jnp.bfloat16)
    scale = 1.0 / math.sqrt(node_count)
    weight_grad = jnp.dot(aggregate.T, pre_grad, preferred_element_type=jnp.float32) * scale
    bias_grad = lax.optimization_barrier(jnp.sum(pre_grad.astype(jnp.float32), axis=0)) * scale
    return (activations, feature_grad, weight_grad, bias_grad)
```

```python
import functools
import math

import jax
import jax.numpy as jnp
from jax import lax
from jax.experimental import pallas as pl
from jax.experimental.pallas import tpu as pltpu
from jax.sharding import PartitionSpec as P

MESH = pl.DeviceIdType.MESH
PLANE = 4
F32, BF16 = jnp.float32, jnp.bfloat16
NT = (((1,), (1,)), ((), ()))
TN = (((0,), (0,)), ((), ()))


def remote(src, dst, send_sem, recv_sem, device):
    return pltpu.make_async_remote_copy(
        src_ref=src, dst_ref=dst, send_sem=send_sem, recv_sem=recv_sem,
        device_id=device, device_id_type=MESH,
    )


def kernel(
    n, scale,
    cols_ref, live_ref, feat_hbm, tiles_hbm, w_ref, b_ref, cot_hbm,
    act_ref, fg_ref, wg_ref, bg_ref,
    feat, tiles, tiles_t, band, band_t, cot, eff, acc,
    p_send, p_recv, agg_grad, s_send, s_recv, t_send, t_recv,
    w_send, w_recv, z_recv, g_send, g_recv,
    local_sem, f_ssem, f_rsem, p_ssem, p_rsem, s_ssem, s_rsem, t_ssem, t_rsem,
    w_ssem, w_rsem, z_ssem, z_rsem, g_ssem, g_rsem,
):
    me, rep = lax.axis_index("rows"), lax.axis_index("rep")
    nb, slots, tile = tiles_hbm.shape[0], tiles_hbm.shape[1], tiles_hbm.shape[2]
    rows = nb * tile
    width = w_ref.shape[0]
    groups = n // PLANE
    quad = lax.rem(me, PLANE)
    layer = lax.div(me, PLANE)
    has_low, has_high = me > 0, me < n - 1
    low, high = (me - 1, rep), (me + 1, rep)
    partner = (me, 1 - rep)
    chunk = 2 * tile
    chunks = rows // chunk

    def plane_peer(d):
        return lax.rem(quad + d, PLANE)

    def layer_peer(d):
        return lax.rem(layer + d, groups)

    barrier = pltpu.get_barrier_semaphore()

    def greet(device):
        pl.semaphore_signal(barrier, inc=1, device_id=device, device_id_type=MESH)

    @pl.when(has_low)
    def _():
        greet(low)

    @pl.when(has_high)
    def _():
        greet(high)

    greet(partner)
    for d in range(1, PLANE):
        greet((layer * PLANE + plane_peer(d), rep))
    for d in range(1, groups):
        greet((layer_peer(d) * PLANE + quad, rep))

    tiles_in = pltpu.make_async_copy(
        tiles_hbm, tiles.at[pl.ds(0, nb)], local_sem.at[0]
    )
    feat_in = pltpu.make_async_copy(feat_hbm, feat.at[1], local_sem.at[1])
    cot_in = pltpu.make_async_copy(cot_hbm, cot, local_sem.at[2])
    tiles_in.start()
    feat_in.start()
    cot_in.start()

    pl.semaphore_wait(
        barrier, PLANE + groups - 1 + has_low.astype(jnp.int32) + has_high.astype(jnp.int32)
    )

    def feat_copy(j, up):
        piece = pl.ds(j * chunk, chunk)
        return remote(
            feat_hbm.at[piece], feat.at[0 if up else 2, piece],
            f_ssem.at[int(up), j], f_rsem.at[int(up), j], high if up else low,
        )

    @pl.when(has_high)
    def _():
        for j in range(chunks):
            feat_copy(j, True).start()

    @pl.when(has_low)
    def _():
        for j in range(chunks):
            feat_copy(j, False).start()

    @pl.when(jnp.logical_not(has_low))
    def _():
        feat[0] = jnp.zeros(feat.shape[1:], BF16)
        s_recv[0] = jnp.zeros(s_recv.shape[1:], BF16)

    @pl.when(jnp.logical_not(has_high))
    def _():
        feat[2] = jnp.zeros(feat.shape[1:], BF16)
        s_recv[1] = jnp.zeros(s_recv.shape[1:], BF16)

    first = (me - 1) * nb
    for g in range(nb):
        count = live_ref[g, 0]
        for k in range(slots):
            eff[g * slots + k] = jnp.where(k < count, cols_ref[g, k] - first, -1)

    tiles[nb, 0] = jnp.zeros((tile, tile), BF16)
    tiles_t[nb, 0] = jnp.zeros((tile, tile), BF16)
    tiles_in.wait()

    def flip(g, carry):
        for k in range(slots):
            tiles_t[g, k] = tiles[g, k].T
        return carry

    lax.fori_loop(0, nb, flip, 0)

    def place(s, carry):
        at = pl.ds(pl.multiple_of(s * tile, tile), tile)
        for g in range(nb):
            a, k_at = jnp.int32(nb), jnp.int32(0)
            for k in range(slots):
                hit = eff[g * slots + k] == s
                a = jnp.where(hit, g, a)
                k_at = jnp.where(hit, k, k_at)
            band[g * tile:(g + 1) * tile, at] = tiles[a, k_at]
            band_t[at, g * tile:(g + 1) * tile] = tiles_t[a, k_at]
        return carry

    lax.fori_loop(0, 3 * nb, place, 0)
    feat_in.wait()

    def dot(a, b):
        return jnp.dot(a, b, preferred_element_type=F32)

    def own_rows(m, carry):
        at = pl.ds(pl.multiple_of(m * chunk, chunk), chunk)
        acc[at, :] = dot(band[at, rows:2 * rows], feat[1])
        return carry

    lax.fori_loop(0, chunks, own_rows, 0)

    @pl.when(has_low)
    def _():
        for j in range(chunks):
            feat_copy(j, True).wait_recv()

    def low_rows(m, carry):
        at = pl.ds(pl.multiple_of(m * chunk, chunk), chunk)
        acc[at, :] += dot(band[at, :rows], feat[0])
        return carry

    lax.fori_loop(0, chunks, low_rows, 0)

    @pl.when(has_high)
    def _():
        for j in range(chunks):
            feat_copy(j, False).wait_recv()

    def p_copy(m):
        return remote(p_send.at[m], p_recv.at[m], p_ssem.at[m], p_rsem.at[m], partner)

    for m in range(chunks):
        at = pl.ds(m * chunk, chunk)
        p_send[m] = (acc[at, :] + dot(band[at, 2 * rows:], feat[2])).astype(BF16)
        p_copy(m).start()
    cot_in.wait()

    w = w_ref[...]
    w_part = jnp.zeros((width, width), F32)
    b_part = jnp.zeros((1, width), F32)
    for m in range(chunks):
        at = pl.ds(m * chunk, chunk)
        p_copy(m).wait_recv()
        agg = (p_send[m].astype(F32) + p_recv[m].astype(F32)).astype(BF16)
        pre = dot(agg, w) + b_ref[...]
        sig = jax.nn.sigmoid(pre)
        act_ref[at, :] = (pre * sig).astype(BF16)
        pre_grad = (cot[at, :].astype(F32) * sig * (1.0 + pre * (1.0 - sig))).astype(BF16)
        agg_grad[at, :] = lax.dot_general(
            pre_grad, w, NT, preferred_element_type=F32
        ).astype(BF16)
        w_part += lax.dot_general(agg, pre_grad, TN, preferred_element_type=F32)
        b_part += jnp.sum(pre_grad.astype(F32), axis=0, keepdims=True)

    part = width // PLANE
    for c in range(PLANE):
        w_send[c, :part] = w_part[c * part:(c + 1) * part].astype(BF16)
        w_send[c, part:] = jnp.broadcast_to(b_part, (16, width)).astype(BF16)

    def w_copy(d, slot):
        peer = plane_peer(d)
        return remote(
            w_send.at[peer], w_recv.at[slot], w_ssem.at[d - 1], w_rsem.at[d - 1],
            (layer * PLANE + peer, rep),
        )

    for d in range(1, PLANE):
        w_copy(d, quad).start()
    w_recv[quad] = w_send[quad]

    def s_copy(j, up):
        return remote(
            s_send.at[int(up), j], s_recv.at[1 - int(up) if not up else 0, j],
            s_ssem.at[int(up), j], s_rsem.at[int(up), j], high if up else low,
        )

    for j in range(chunks):
        s_send[1, j] = dot(
            band_t[2 * rows + j * chunk:2 * rows + (j + 1) * chunk, :], agg_grad[...]
        ).astype(BF16)

        @pl.when(has_high)
        def _():
            s_copy(j, True).start()

        s_send[0, j] = dot(
            band_t[j * chunk:(j + 1) * chunk, :], agg_grad[...]
        ).astype(BF16)

        @pl.when(has_low)
        def _():
            s_copy(j, False).start()

    for d in range(1, PLANE):
        w_copy(d, lax.rem(quad + PLANE - d, PLANE)).wait_recv()
    z_recv[layer] = sum(w_recv[c].astype(F32) for c in range(PLANE)).astype(BF16)

    def z_copy(d, slot):
        return remote(
            z_recv.at[layer], z_recv.at[slot], z_ssem.at[d - 1], z_rsem.at[d - 1],
            (layer_peer(d) * PLANE + quad, rep),
        )

    for d in range(1, groups):
        z_copy(d, layer).start()

    def own_terms(m, carry):
        at = pl.ds(pl.multiple_of(m * chunk, chunk), chunk)
        own = pl.ds(pl.multiple_of(rows + m * chunk, chunk), chunk)
        acc[at, :] = dot(band_t[own, :], agg_grad[...])
        return carry

    lax.fori_loop(0, chunks, own_terms, 0)

    def t_copy(m):
        return remote(t_send.at[m], t_recv.at[m], t_ssem.at[m], t_rsem.at[m], partner)

    for m in range(chunks):
        @pl.when(has_low)
        def _():
            s_copy(m, True).wait_recv()

        @pl.when(has_high)
        def _():
            s_copy(m, False).wait_recv()

        t_send[m] = (
            acc[m * chunk:(m + 1) * chunk, :] + s_recv[0, m].astype(F32) + s_recv[1, m].astype(F32)
        ).astype(BF16)
        t_copy(m).start()

    for d in range(1, groups):
        z_copy(d, lax.rem(layer + groups - d, groups)).wait_recv()
    total = sum(z_recv[c].astype(F32) for c in range(groups)) * scale
    bg_ref[...] = total[part:part + 1]
    g_send[...] = total[:part]
    g_recv[quad] = total[:part]

    def g_copy(d, slot):
        return remote(
            g_send, g_recv.at[slot], g_ssem.at[d - 1], g_rsem.at[d - 1],
            (layer * PLANE + plane_peer(d), rep),
        )

    for d in range(1, PLANE):
        g_copy(d, quad).start()

    for m in range(chunks):
        t_copy(m).wait_recv()
        fg_ref[m * chunk:(m + 1) * chunk, :] = (
            t_send[m].astype(F32) + t_recv[m].astype(F32)
        ).astype(BF16)

    for d in range(1, PLANE):
        g_copy(d, lax.rem(quad + PLANE - d, PLANE)).wait_recv()
    for c in range(PLANE):
        wg_ref[c * part:(c + 1) * part, :] = g_recv[c]

    @pl.when(has_high)
    def _():
        for j in range(chunks):
            feat_copy(j, True).wait_send()
            s_copy(j, True).wait_send()

    @pl.when(has_low)
    def _():
        for j in range(chunks):
            feat_copy(j, False).wait_send()
            s_copy(j, False).wait_send()

    for m in range(chunks):
        p_copy(m).wait_send()
        t_copy(m).wait_send()
    for d in range(1, PLANE):
        w_copy(d, quad).wait_send()
        g_copy(d, quad).wait_send()
    for d in range(1, groups):
        z_copy(d, layer).wait_send()


def solution(mesh):
    n = mesh.shape["rows"]

    def local(features, tiles, columns, live, weight, bias, cotangent):
        nb, slots, tile, _ = tiles.shape
        rows, width = features.shape
        chunk = 2 * tile
        chunks = rows // chunk
        groups = n // PLANE
        part = width // PLANE
        vmem, dma = pltpu.VMEM, pltpu.SemaphoreType.DMA
        any_, whole = pl.BlockSpec(memory_space=pl.ANY), pl.BlockSpec(memory_space=pltpu.VMEM)
        smem = pl.BlockSpec(memory_space=pltpu.SMEM)
        act, feature_grad, weight_grad, bias_grad = pl.pallas_call(
            functools.partial(kernel, n, 1.0 / math.sqrt(rows * n)),
            out_shape=(
                jax.ShapeDtypeStruct((rows, width), BF16),
                jax.ShapeDtypeStruct((rows, width), BF16),
                jax.ShapeDtypeStruct((width, width), F32),
                jax.ShapeDtypeStruct((1, width), F32),
            ),
            in_specs=[smem, smem, any_, any_, whole, whole, any_],
            out_specs=(whole, whole, whole, whole),
            scratch_shapes=[
                vmem((3, rows, width), BF16),
                vmem((nb + 1, slots, tile, tile), BF16),
                vmem((nb + 1, slots, tile, tile), BF16),
                vmem((rows, 3 * rows), BF16),
                vmem((3 * rows, rows), BF16),
                vmem((rows, width), BF16),
                pltpu.SMEM((nb * slots,), jnp.int32),
                vmem((rows, width), F32),
                vmem((chunks, chunk, width), BF16),
                vmem((chunks, chunk, width), BF16),
                vmem((rows, width), BF16),
                vmem((2, chunks, chunk, width), BF16),
                vmem((2, chunks, chunk, width), BF16),
                vmem((chunks, chunk, width), BF16),
                vmem((chunks, chunk, width), BF16),
                vmem((PLANE, part + 16, width), BF16),
                vmem((PLANE, part + 16, width), BF16),
                vmem((groups, part + 16, width), BF16),
                vmem((part, width), F32),
                vmem((PLANE, part, width), F32),
                dma((3,)),
                dma((2, chunks)), dma((2, chunks)),
                dma((chunks,)), dma((chunks,)),
                dma((2, chunks)), dma((2, chunks)),
                dma((chunks,)), dma((chunks,)),
                dma((PLANE - 1,)), dma((PLANE - 1,)),
                dma((groups - 1,)), dma((groups - 1,)),
                dma((PLANE - 1,)), dma((PLANE - 1,)),
            ],
            compiler_params=pltpu.CompilerParams(
                collective_id=0, has_side_effects=True, vmem_limit_bytes=48 * 2**20
            ),
        )(columns, live, features, tiles, weight, bias.reshape(1, width), cotangent)
        return act, feature_grad, weight_grad, bias_grad.reshape(width)

    return jax.shard_map(
        local,
        mesh=mesh,
        in_specs=(
            P("rows", None), P("rows", "rep", None, None), P("rows", "rep"), P("rows", "rep"),
            P(), P(), P("rows", None),
        ),
        out_specs=(P("rows", None), P("rows", None), P(), P()),
        check_vma=False,
    )
```

```python
import functools
import math

import jax
import jax.numpy as jnp
from jax import lax
from jax.experimental import pallas as pl
from jax.experimental.pallas import tpu as pltpu
from jax.sharding import PartitionSpec as P

MESH = pl.DeviceIdType.MESH
PLANE = 4
F32, BF16 = jnp.float32, jnp.bfloat16
NT = (((1,), (1,)), ((), ()))
TN = (((0,), (0,)), ((), ()))


def remote(src, dst, send_sem, recv_sem, device):
    return pltpu.make_async_remote_copy(
        src_ref=src, dst_ref=dst, send_sem=send_sem, recv_sem=recv_sem,
        device_id=device, device_id_type=MESH,
    )


def kernel(
    n, scale,
    cols_hbm, live_hbm, feat_hbm, tiles_hbm, w_hbm, b_hbm, cot_hbm,
    act_hbm, fg_hbm, wg_hbm, bg_hbm,
    act_ref, fg_ref, wg_ref, bg_ref, cols, live, w_ref, b_ref, feat, tiles, tiles_t, band, band_t, cot, eff, acc,
    p_send, p_recv, agg_all, grad_all, agg_grad, s_send, s_recv, t_send, t_recv,
    w_send, w_recv, z_recv, g_send, g_recv,
    local_sem, out_sem, f_ssem, f_rsem, p_ssem, p_rsem, s_ssem, s_rsem, t_ssem, t_rsem,
    w_ssem, w_rsem, z_ssem, z_rsem, g_ssem, g_rsem,
):
    me, rep = lax.axis_index("rows"), lax.axis_index("rep")
    nb, slots, tile = tiles_hbm.shape[0], tiles_hbm.shape[1], tiles_hbm.shape[2]
    rows = nb * tile
    width = w_hbm.shape[0]
    groups = n // PLANE
    quad = lax.rem(me, PLANE)
    layer = lax.div(me, PLANE)
    chunk = 2 * tile
    chunks = rows // chunk
    even = lax.rem(me, 2) == 0
    near = jnp.where(even, me + 1, me - 1)
    far = jnp.where(even, me - 1, me + 1)
    has_far = jnp.logical_and(far >= 0, far < n)
    partner = (me, 1 - rep)

    def plane_peer(d):
        return lax.rem(quad + d, PLANE)

    def layer_peer(d):
        return lax.rem(layer + d, groups)

    barrier = pltpu.get_barrier_semaphore()

    def greet(device):
        pl.semaphore_signal(barrier, inc=1, device_id=device, device_id_type=MESH)

    @pl.when(has_far)
    def _():
        greet((far, rep))

    greet((near, rep))
    greet(partner)
    for d in range(1, PLANE):
        greet((layer * PLANE + plane_peer(d), rep))
    for d in range(1, groups):
        greet((layer_peer(d) * PLANE + quad, rep))

    loads = [
        pltpu.make_async_copy(src, dst, local_sem.at[i])
        for i, (src, dst) in enumerate((
            (cols_hbm, cols), (live_hbm, live), (tiles_hbm, tiles.at[pl.ds(0, nb)]),
            (feat_hbm, feat.at[pl.ds(rows, rows)]), (w_hbm, w_ref), (b_hbm, b_ref),
            (cot_hbm, cot),
        ))
    ]
    for load in loads:
        load.start()

    pl.semaphore_wait(barrier, PLANE + groups + has_far.astype(jnp.int32))

    def far_feat(j):
        start = pl.multiple_of(jnp.where(even, j, chunks - 1 - j) * chunk, chunk)
        return remote(
            feat_hbm.at[pl.ds(start, chunk)], feat.at[pl.ds(j * chunk, chunk)],
            f_ssem.at[j], f_rsem.at[j], (far, rep),
        )

    near_feat = remote(
        feat_hbm, feat.at[pl.ds(2 * rows, rows)],
        f_ssem.at[chunks], f_rsem.at[chunks], (near, rep),
    )

    @pl.when(has_far)
    def _():
        for j in range(chunks):
            far_feat(j).start()

    near_feat.start()

    @pl.when(jnp.logical_not(has_far))
    def _():
        feat[:rows] = jnp.zeros((rows, width), BF16)
        s_recv[0] = jnp.zeros(s_recv.shape[1:], BF16)

    tiles[nb, 0] = jnp.zeros((tile, tile), BF16)
    tiles_t[nb, 0] = jnp.zeros((tile, tile), BF16)

    first = (me - 1) * nb
    loads[0].wait()
    loads[1].wait()
    for g in range(nb):
        count = live[0, g]
        for k in range(slots):
            block = cols[g, k] - first
            pair = lax.div(block, 2)
            turned = block + 2 * (nb // 2 - 1 - 2 * pair)
            from_even = jnp.where(block < nb, turned, block)
            from_odd = jnp.where(
                block < nb, block + 2 * nb, jnp.where(block < 2 * nb, block, block - 2 * nb)
            )
            eff[g * slots + k] = jnp.where(
                k < count, jnp.where(even, from_even, from_odd), -1
            )
    loads[2].wait()

    def slot_of(g, s):
        a, k_at = jnp.int32(nb), jnp.int32(0)
        for k in range(slots):
            hit = eff[g * slots + k] == s
            a = jnp.where(hit, g, a)
            k_at = jnp.where(hit, k, k_at)
        return a, k_at

    def place(s, carry):
        at = pl.ds(pl.multiple_of(s * tile, tile), tile)
        for g in range(nb):
            a, k_at = slot_of(g, s)
            band[g * tile:(g + 1) * tile, at] = tiles[a, k_at]
        return carry

    lax.fori_loop(0, 3 * nb, place, 0)

    def dot(a, b):
        return jnp.dot(a, b, preferred_element_type=F32)

    def chunk_at(m):
        return pl.ds(pl.multiple_of(m * chunk, chunk), chunk)

    loads[3].wait()
    near_feat.wait_recv()

    def near_rows(m, carry):
        acc[chunk_at(m), :] = dot(band[chunk_at(m), rows:], feat[rows:])
        return carry

    lax.fori_loop(0, chunks, near_rows, 0)

    def p_copy(j):
        return remote(p_send.at[j], p_recv.at[j], p_ssem.at[j], p_rsem.at[j], partner)

    def forward_chunk(j):
        return jnp.where(even, chunks - 1 - j, j)

    for j in range(chunks):
        @pl.when(has_far)
        def _():
            far_feat(j).wait_recv()

        at, reach = chunk_at(forward_chunk(j)), (j + 1) * chunk
        p_send[j] = (acc[at, :] + dot(band[at, :reach], feat[:reach])).astype(BF16)
        p_copy(j).start()

    def flip(g, carry):
        for k in range(slots):
            tiles_t[g, k] = tiles[g, k].T
        return carry

    lax.fori_loop(0, nb, flip, 0)

    def place_t(s, carry):
        at = pl.ds(pl.multiple_of(s * tile, tile), tile)
        for g in range(nb):
            a, k_at = slot_of(g, s)
            band_t[at, g * tile:(g + 1) * tile] = tiles_t[a, k_at]
        return carry

    lax.fori_loop(0, 3 * nb, place_t, 0)

    for load in loads[4:]:
        load.wait()
    for j in range(chunks):
        at = chunk_at(forward_chunk(j))
        p_copy(j).wait_recv()
        agg = (p_send[j].astype(F32) + p_recv[j].astype(F32)).astype(BF16)
        pre = dot(agg, w_ref[...]) + b_ref[...]
        sig = jax.nn.sigmoid(pre)
        pre_grad = (cot[at, :].astype(F32) * sig * (1.0 + pre * (1.0 - sig))).astype(BF16)
        agg_grad[at, :] = lax.dot_general(
            pre_grad, w_ref[...], NT, preferred_element_type=F32
        ).astype(BF16)
        act_ref[at, :] = (pre * sig).astype(BF16)
        agg_all[at, :] = agg
        grad_all[at, :] = pre_grad
    act_out = pltpu.make_async_copy(act_ref, act_hbm, out_sem.at[chunks])
    act_out.start()

    def far_copy(j):
        return remote(
            s_send.at[0, j], s_recv.at[0, j], s_ssem.at[j], s_rsem.at[j], (far, rep)
        )

    near_copy = remote(
        s_send.at[1], s_recv.at[1], s_ssem.at[chunks], s_rsem.at[chunks], (near, rep)
    )

    for j in range(chunks):
        s_send[0, j] = dot(band_t[j * chunk:(j + 1) * chunk, :], agg_grad[...]).astype(BF16)

        @pl.when(has_far)
        def _():
            far_copy(j).start()

    part = width // PLANE
    w_part = lax.dot_general(agg_all[...], grad_all[...], TN, preferred_element_type=F32)
    b_part = jnp.sum(grad_all[...].astype(F32), axis=0, keepdims=True)
    for c in range(PLANE):
        w_send[c, :part] = w_part[c * part:(c + 1) * part].astype(BF16)
        w_send[c, part:] = jnp.broadcast_to(b_part, (16, width)).astype(BF16)

    def w_copy(d, slot):
        peer = plane_peer(d)
        return remote(
            w_send.at[peer], w_recv.at[slot], w_ssem.at[d - 1], w_rsem.at[d - 1],
            (layer * PLANE + peer, rep),
        )

    for d in range(1, PLANE):
        w_copy(d, quad).start()
    w_recv[quad] = w_send[quad]

    def near_terms(m, carry):
        at = pl.ds(pl.multiple_of(2 * rows + m * chunk, chunk), chunk)
        s_send[1, m] = dot(band_t[at, :], agg_grad[...]).astype(BF16)
        return carry

    lax.fori_loop(0, chunks, near_terms, 0)
    near_copy.start()

    def own_terms(m, carry):
        at = pl.ds(pl.multiple_of(rows + m * chunk, chunk), chunk)
        acc[chunk_at(m), :] = dot(band_t[at, :], agg_grad[...])
        return carry

    lax.fori_loop(0, chunks, own_terms, 0)

    def t_copy(j):
        return remote(t_send.at[j], t_recv.at[j], t_ssem.at[j], t_rsem.at[j], partner)

    def z_copy(d, slot):
        return remote(
            z_recv.at[layer], z_recv.at[slot], z_ssem.at[d - 1], z_rsem.at[d - 1],
            (layer_peer(d) * PLANE + quad, rep),
        )

    def backward_chunk(j):
        return jnp.where(even, j, chunks - 1 - j)

    near_copy.wait_recv()
    for j in range(chunks):
        @pl.when(has_far)
        def _():
            far_copy(j).wait_recv()

        m = backward_chunk(j)
        t_send[j] = (
            acc[chunk_at(m), :] + s_recv[0, j].astype(F32) + s_recv[1, m].astype(F32)
        ).astype(BF16)
        t_copy(j).start()
        if j == 0:
            for d in range(1, PLANE):
                w_copy(d, lax.rem(quad + PLANE - d, PLANE)).wait_recv()
            z_recv[layer] = sum(w_recv[c].astype(F32) for c in range(PLANE)).astype(BF16)
            for d in range(1, groups):
                z_copy(d, layer).start()

    for d in range(1, groups):
        z_copy(d, lax.rem(layer + groups - d, groups)).wait_recv()
    total = sum(z_recv[c].astype(F32) for c in range(groups)) * scale
    bg_ref[...] = total[part:part + 1]
    bg_out = pltpu.make_async_copy(bg_ref, bg_hbm, out_sem.at[chunks + 1])
    bg_out.start()
    g_send[...] = total[:part].astype(BF16)
    g_recv[quad] = total[:part].astype(BF16)

    def g_copy(d, slot):
        return remote(
            g_send, g_recv.at[slot], g_ssem.at[d - 1], g_rsem.at[d - 1],
            (layer * PLANE + plane_peer(d), rep),
        )

    for d in range(1, PLANE):
        g_copy(d, quad).start()

    def fg_out(j):
        at = chunk_at(backward_chunk(j))
        return pltpu.make_async_copy(fg_ref.at[at], fg_hbm.at[at], out_sem.at[j])

    for j in range(chunks):
        t_copy(j).wait_recv()
        fg_ref[chunk_at(backward_chunk(j)), :] = (
            t_send[j].astype(F32) + t_recv[j].astype(F32)
        ).astype(BF16)
        fg_out(j).start()

    for d in range(1, PLANE):
        g_copy(d, lax.rem(quad + PLANE - d, PLANE)).wait_recv()
    for c in range(PLANE):
        wg_ref[c * part:(c + 1) * part, :] = g_recv[c].astype(F32)
    wg_out = pltpu.make_async_copy(wg_ref, wg_hbm, out_sem.at[chunks + 2])
    wg_out.start()

    @pl.when(has_far)
    def _():
        for j in range(chunks):
            far_feat(j).wait_send()
            far_copy(j).wait_send()

    near_feat.wait_send()
    near_copy.wait_send()
    for j in range(chunks):
        p_copy(j).wait_send()
        t_copy(j).wait_send()
    for d in range(1, PLANE):
        w_copy(d, quad).wait_send()
        g_copy(d, quad).wait_send()
    for d in range(1, groups):
        z_copy(d, layer).wait_send()

    for j in range(chunks):
        fg_out(j).wait()
    for out in (act_out, bg_out, wg_out):
        out.wait()


def hand_out(*refs):
    count = len(refs) // 2
    copies = [
        pltpu.make_async_copy(refs[i], refs[count + i], refs[-1].at[i]) for i in range(count)
    ]
    for copy in copies:
        copy.start()
    for copy in copies:
        copy.wait()


def solution(mesh):
    n = mesh.shape["rows"]

    def local(features, tiles, columns, live, weight, bias, cotangent):
        nb, slots, tile, _ = tiles.shape
        rows, width = features.shape
        chunk = 2 * tile
        chunks = rows // chunk
        groups = n // PLANE
        part = width // PLANE
        vmem, dma = pltpu.VMEM, pltpu.SemaphoreType.DMA
        hbm = pl.BlockSpec(memory_space=pltpu.HBM)
        shapes = (
            jax.ShapeDtypeStruct((rows, width), BF16),
            jax.ShapeDtypeStruct((rows, width), BF16),
            jax.ShapeDtypeStruct((width, width), F32),
            jax.ShapeDtypeStruct((1, width), F32),
        )
        results = pl.pallas_call(
            functools.partial(kernel, n, 1.0 / math.sqrt(rows * n)),
            out_shape=shapes,
            in_specs=[hbm] * 7,
            out_specs=(hbm,) * 4,
            scratch_shapes=[
                vmem((rows, width), BF16),
                vmem((rows, width), BF16),
                vmem((width, width), F32),
                vmem((1, width), F32),
                pltpu.SMEM((nb, slots), jnp.int32),
                pltpu.SMEM((1, nb), jnp.int32),
                vmem((width, width), BF16),
                vmem((1, width), F32),
                vmem((3 * rows, width), BF16),
                vmem((nb + 1, slots, tile, tile), BF16),
                vmem((nb + 1, slots, tile, tile), BF16),
                vmem((rows, 3 * rows), BF16),
                vmem((3 * rows, rows), BF16),
                vmem((rows, width), BF16),
                pltpu.SMEM((nb * slots,), jnp.int32),
                vmem((rows, width), F32),
                vmem((chunks, chunk, width), BF16),
                vmem((chunks, chunk, width), BF16),
                vmem((rows, width), BF16),
                vmem((rows, width), BF16),
                vmem((rows, width), BF16),
                vmem((2, chunks, chunk, width), BF16),
                vmem((2, chunks, chunk, width), BF16),
                vmem((chunks, chunk, width), BF16),
                vmem((chunks, chunk, width), BF16),
                vmem((PLANE, part + 16, width), BF16),
                vmem((PLANE, part + 16, width), BF16),
                vmem((groups, part + 16, width), BF16),
                vmem((part, width), BF16),
                vmem((PLANE, part, width), BF16),
                dma((7,)),
                dma((chunks + 3,)),
                dma((chunks + 1,)), dma((chunks + 1,)),
                dma((chunks,)), dma((chunks,)),
                dma((chunks + 1,)), dma((chunks + 1,)),
                dma((chunks,)), dma((chunks,)),
                dma((PLANE - 1,)), dma((PLANE - 1,)),
                dma((groups - 1,)), dma((groups - 1,)),
                dma((PLANE - 1,)), dma((PLANE - 1,)),
            ],
            compiler_params=pltpu.CompilerParams(
                collective_id=0, has_side_effects=True, vmem_limit_bytes=64 * 2**20
            ),
        )(columns, live.T, features, tiles, weight, bias.reshape(1, width), cotangent)
        act, feature_grad, weight_grad, bias_grad = pl.pallas_call(
            hand_out,
            out_shape=shapes,
            in_specs=[hbm] * 4,
            out_specs=(hbm,) * 4,
            scratch_shapes=[dma((4,))],
            compiler_params=pltpu.CompilerParams(vmem_limit_bytes=64 * 2**20),
        )(*results)
        return act, feature_grad, weight_grad, bias_grad.reshape(width)

    return jax.shard_map(
        local,
        mesh=mesh,
        in_specs=(
            P("rows", None), P("rows", "rep", None, None), P("rows", "rep"), P("rows", "rep"),
            P(), P(), P("rows", None),
        ),
        out_specs=(P("rows", None), P("rows", None), P(), P()),
        check_vma=False,
    )
```

```python
import functools
import math

import jax
import jax.numpy as jnp
from jax import lax
from jax.experimental import pallas as pl
from jax.experimental.pallas import tpu as pltpu
from jax.sharding import PartitionSpec as P

MESH = pl.DeviceIdType.MESH
PLANE = 4
F32, BF16 = jnp.float32, jnp.bfloat16
NT = (((1,), (1,)), ((), ()))
TN = (((0,), (0,)), ((), ()))


def remote(src, dst, send_sem, recv_sem, device):
    return pltpu.make_async_remote_copy(
        src_ref=src, dst_ref=dst, send_sem=send_sem, recv_sem=recv_sem,
        device_id=device, device_id_type=MESH,
    )


def kernel(
    n, scale,
    cols_hbm, live_hbm, feat_hbm, tiles_hbm, w_hbm, b_hbm, cot_hbm,
    act_hbm, fg_hbm, wg_hbm, bg_hbm,
    act_ref, fg_ref, wg_ref, bg_ref, cols, live, w_ref, b_ref, feat, tiles, tiles_t, band, band_t, cot, eff, acc,
    p_send, p_recv, agg_all, grad_all, agg_grad, s_send, s_recv, t_send, t_recv,
    w_send, w_recv, z_recv, g_send, g_recv,
    local_sem, out_sem, f_ssem, f_rsem, p_ssem, p_rsem, s_ssem, s_rsem, t_ssem, t_rsem,
    w_ssem, w_rsem, z_ssem, z_rsem, g_ssem, g_rsem,
):
    me, rep = lax.axis_index("rows"), lax.axis_index("rep")
    nb, slots, tile = tiles_hbm.shape[0], tiles_hbm.shape[1], tiles_hbm.shape[2]
    rows = nb * tile
    width = w_hbm.shape[0]
    groups = n // PLANE
    quad = lax.rem(me, PLANE)
    layer = lax.div(me, PLANE)
    chunk, chunks = tile, nb
    bulk = 2 * tile
    even = lax.rem(me, 2) == 0
    near = jnp.where(even, me + 1, me - 1)
    far = jnp.where(even, me - 1, me + 1)
    has_far = jnp.logical_and(far >= 0, far < n)
    far_even = jnp.logical_and(has_far, even)
    far_odd = jnp.logical_and(has_far, jnp.logical_not(even))
    partner = (me, 1 - rep)

    def plane_peer(d):
        return lax.rem(quad + d, PLANE)

    def layer_peer(d):
        return lax.rem(layer + d, groups)

    barrier = pltpu.get_barrier_semaphore()

    def greet(device):
        pl.semaphore_signal(barrier, inc=1, device_id=device, device_id_type=MESH)

    @pl.when(has_far)
    def _():
        greet((far, rep))

    greet((near, rep))
    greet(partner)
    for d in range(1, PLANE):
        greet((layer * PLANE + plane_peer(d), rep))
        greet((layer * PLANE + plane_peer(d), 1 - rep))
    for d in range(1, groups):
        greet((layer_peer(d) * PLANE + quad, rep))

    loads = [
        pltpu.make_async_copy(src, dst, local_sem.at[i])
        for i, (src, dst) in enumerate((
            (cols_hbm, cols), (live_hbm, live), (tiles_hbm, tiles.at[pl.ds(0, nb)]),
            (feat_hbm, feat.at[pl.ds(rows, rows)]), (w_hbm, w_ref), (b_hbm, b_ref),
            (cot_hbm, cot),
        ))
    ]
    for load in loads:
        load.start()

    loads[3].wait()
    pl.semaphore_wait(barrier, 2 * PLANE - 1 + groups + has_far.astype(jnp.int32))

    def far_feat(j):
        start = pl.multiple_of(jnp.where(even, j, chunks - 1 - j) * chunk, chunk)
        return remote(
            feat.at[pl.ds(rows + start, chunk)], feat.at[pl.ds(j * chunk, chunk)],
            f_ssem.at[j], f_rsem.at[j], (far, rep),
        )

    near_feat = remote(
        feat.at[pl.ds(rows, rows)], feat.at[pl.ds(2 * rows, rows)],
        f_ssem.at[chunks], f_rsem.at[chunks], (near, rep),
    )

    for j in range(chunks):
        @pl.when(has_far if j < chunks - 1 else far_odd)
        def _():
            far_feat(j).start()

    near_feat.start()
    last = (chunks - 1) * chunk

    @pl.when(jnp.logical_not(has_far))
    def _():
        feat[:last] = jnp.zeros((last, width), BF16)
        s_recv[0, :last] = jnp.zeros((last, width), BF16)

    @pl.when(jnp.logical_not(far_even))
    def _():
        feat[last:rows] = jnp.zeros((chunk, width), BF16)

    @pl.when(jnp.logical_not(far_odd))
    def _():
        s_recv[0, last:] = jnp.zeros((chunk, width), BF16)

    tiles[nb, 0] = jnp.zeros((tile, tile), BF16)
    tiles_t[nb, 0] = jnp.zeros((tile, tile), BF16)

    first = (me - 1) * nb
    loads[0].wait()
    loads[1].wait()
    for g in range(nb):
        count = live[0, g]
        for k in range(slots):
            block = cols[g, k] - first
            from_even = jnp.where(block < nb, nb - 1 - block, block)
            from_odd = jnp.where(
                block < nb, block + 2 * nb, jnp.where(block < 2 * nb, block, block - 2 * nb)
            )
            eff[g * slots + k] = jnp.where(
                k < count, jnp.where(even, from_even, from_odd), -1
            )
    loads[2].wait()

    def slot_of(g, s):
        a, k_at = jnp.int32(nb), jnp.int32(0)
        for k in range(slots):
            hit = eff[g * slots + k] == s
            a = jnp.where(hit, g, a)
            k_at = jnp.where(hit, k, k_at)
        return a, k_at

    def place(s, carry):
        at = pl.ds(pl.multiple_of(s * tile, tile), tile)
        for g in range(nb):
            a, k_at = slot_of(g, s)
            band[g * tile:(g + 1) * tile, at] = tiles[a, k_at]
        return carry

    lax.fori_loop(0, 3 * nb, place, 0)

    def dot(a, b):
        return jnp.dot(a, b, preferred_element_type=F32)

    def chunk_at(m):
        return pl.ds(pl.multiple_of(m * chunk, chunk), chunk)

    def bulk_at(m):
        return pl.ds(pl.multiple_of(m * bulk, bulk), bulk)

    near_feat.wait_recv()

    def near_rows(m, carry):
        acc[bulk_at(m), :] = dot(band[bulk_at(m), rows:], feat[rows:])
        return carry

    lax.fori_loop(0, rows // bulk, near_rows, 0)

    def p_copy(j):
        return remote(p_send.at[j], p_recv.at[j], p_ssem.at[j], p_rsem.at[j], partner)

    def forward_chunk(j):
        return jnp.where(even, chunks - 1 - j, j)

    def flip(g, carry):
        for k in range(slots):
            tiles_t[g, k] = tiles[g, k].T
        return carry

    def place_t(s, carry):
        at = pl.ds(pl.multiple_of(s * tile, tile), tile)
        for g in range(nb):
            a, k_at = slot_of(g, s)
            band_t[at, g * tile:(g + 1) * tile] = tiles_t[a, k_at]
        return carry

    for j in range(chunks):
        @pl.when(has_far if j < chunks - 1 else far_even)
        def _():
            far_feat(j).wait_recv()

        at, reach = chunk_at(forward_chunk(j)), (j + 1) * chunk
        p_send[j] = (acc[at, :] + dot(band[at, :reach], feat[:reach])).astype(BF16)
        p_copy(j).start()
        if j < 3:
            lax.fori_loop(j * nb // 3, (j + 1) * nb // 3, flip, 0)
        elif j < 5:
            lax.fori_loop(6 * nb // 4 * (j - 3), 6 * nb // 4 * (j - 2), place_t, 0)

    for load in loads[4:]:
        load.wait()
    for j in range(chunks):
        at = chunk_at(forward_chunk(j))
        p_copy(j).wait_recv()
        agg = (p_send[j].astype(F32) + p_recv[j].astype(F32)).astype(BF16)
        pre = dot(agg, w_ref[...]) + b_ref[...]
        sig = jax.nn.sigmoid(pre)
        pre_grad = (cot[at, :].astype(F32) * sig * (1.0 + pre * (1.0 - sig))).astype(BF16)
        agg_grad[at, :] = lax.dot_general(
            pre_grad, w_ref[...], NT, preferred_element_type=F32
        ).astype(BF16)
        act_ref[at, :] = (pre * sig).astype(BF16)
        agg_all[at, :] = agg
        grad_all[at, :] = pre_grad
    act_out = pltpu.make_async_copy(act_ref, act_hbm, out_sem.at[chunks])
    act_out.start()

    def far_copy(j):
        piece = pl.ds(j * chunk, chunk)
        return remote(
            s_send.at[0, piece], s_recv.at[0, piece], s_ssem.at[j], s_rsem.at[j], (far, rep)
        )

    near_copy = remote(
        s_send.at[1], s_recv.at[1], s_ssem.at[chunks], s_rsem.at[chunks], (near, rep)
    )

    def far_terms(j):
        at = slice(j * chunk, (j + 1) * chunk)
        s_send[0, at] = dot(band_t[at, :], agg_grad[...]).astype(BF16)

        @pl.when(has_far if j < chunks - 1 else far_even)
        def _():
            far_copy(j).start()

    for j in range(chunks // 2):
        far_terms(j)

    half = width // 2
    part = half // PLANE
    mine = pl.ds(pl.multiple_of(rep * half, half), half)
    w_part = lax.dot_general(agg_all[:, mine], grad_all[...], TN, preferred_element_type=F32)
    b_part = jnp.sum(grad_all[...].astype(F32), axis=0, keepdims=True)
    for c in range(PLANE):
        w_send[c, :part] = w_part[c * part:(c + 1) * part].astype(BF16)
        w_send[c, part:] = jnp.broadcast_to(b_part, (16, width)).astype(BF16)

    def w_copy(d, slot):
        peer = plane_peer(d)
        return remote(
            w_send.at[peer], w_recv.at[slot], w_ssem.at[d - 1], w_rsem.at[d - 1],
            (layer * PLANE + peer, rep),
        )

    for d in range(1, PLANE):
        w_copy(d, quad).start()
    w_recv[quad] = w_send[quad]

    for j in range(chunks // 2, chunks):
        far_terms(j)

    def near_terms(m, carry):
        at = pl.ds(pl.multiple_of(2 * rows + m * bulk, bulk), bulk)
        s_send[1, bulk_at(m)] = dot(band_t[at, :], agg_grad[...]).astype(BF16)
        return carry

    lax.fori_loop(0, rows // bulk, near_terms, 0)
    near_copy.start()

    def own_terms(m, carry):
        at = pl.ds(pl.multiple_of(rows + m * bulk, bulk), bulk)
        acc[bulk_at(m), :] = dot(band_t[at, :], agg_grad[...])
        return carry

    lax.fori_loop(0, rows // bulk, own_terms, 0)

    def t_copy(j):
        return remote(t_send.at[j], t_recv.at[j], t_ssem.at[j], t_rsem.at[j], partner)

    def z_copy(d, slot):
        return remote(
            z_recv.at[layer], z_recv.at[slot], z_ssem.at[d - 1], z_rsem.at[d - 1],
            (layer_peer(d) * PLANE + quad, rep),
        )

    def backward_chunk(j):
        return jnp.where(even, j, chunks - 1 - j)

    near_copy.wait_recv()
    for j in range(chunks):
        @pl.when(has_far if j < chunks - 1 else far_odd)
        def _():
            far_copy(j).wait_recv()

        at = chunk_at(backward_chunk(j))
        t_send[j] = (
            acc[at, :] + s_recv[0, j * chunk:(j + 1) * chunk].astype(F32)
            + s_recv[1, at].astype(F32)
        ).astype(BF16)
        t_copy(j).start()
        if j == 1:
            for d in range(1, PLANE):
                w_copy(d, lax.rem(quad + PLANE - d, PLANE)).wait_recv()
            z_recv[layer] = sum(w_recv[c].astype(F32) for c in range(PLANE)).astype(BF16)
            for d in range(1, groups):
                z_copy(d, layer).start()

    for d in range(1, groups):
        z_copy(d, lax.rem(layer + groups - d, groups)).wait_recv()
    total = sum(z_recv[c].astype(F32) for c in range(groups)) * scale
    bg_ref[...] = total[part:part + 1]
    bg_out = pltpu.make_async_copy(bg_ref, bg_hbm, out_sem.at[chunks + 1])
    bg_out.start()
    g_send[...] = total[:part].astype(BF16)
    g_recv[rep * PLANE + quad] = total[:part].astype(BF16)

    def g_copy(turn, d, slot):
        at = turn * PLANE + d - 1
        return remote(
            g_send, g_recv.at[slot], g_ssem.at[at], g_rsem.at[at],
            (layer * PLANE + plane_peer(d), 1 - rep if turn else rep),
        )

    others = [(turn, d) for turn in range(2) for d in range(PLANE) if turn or d]
    for turn, d in others:
        g_copy(turn, d, rep * PLANE + quad).start()

    def fg_out(j):
        at = chunk_at(backward_chunk(j))
        return pltpu.make_async_copy(fg_ref.at[at], fg_hbm.at[at], out_sem.at[j])

    for j in range(chunks):
        t_copy(j).wait_recv()
        fg_ref[chunk_at(backward_chunk(j)), :] = (
            t_send[j].astype(F32) + t_recv[j].astype(F32)
        ).astype(BF16)
        fg_out(j).start()

    for turn, d in others:
        source = lax.rem(quad + PLANE - d, PLANE)
        g_copy(turn, d, (1 - rep if turn else rep) * PLANE + source).wait_recv()
    for c in range(2 * PLANE):
        wg_ref[c * part:(c + 1) * part, :] = g_recv[c].astype(F32)
    wg_out = pltpu.make_async_copy(wg_ref, wg_hbm, out_sem.at[chunks + 2])
    wg_out.start()

    for j in range(chunks):
        @pl.when(has_far if j < chunks - 1 else far_odd)
        def _():
            far_feat(j).wait_send()

        @pl.when(has_far if j < chunks - 1 else far_even)
        def _():
            far_copy(j).wait_send()

    near_feat.wait_send()
    near_copy.wait_send()
    for j in range(chunks):
        p_copy(j).wait_send()
        t_copy(j).wait_send()
    for d in range(1, PLANE):
        w_copy(d, quad).wait_send()
    for turn, d in others:
        g_copy(turn, d, rep * PLANE + quad).wait_send()
    for d in range(1, groups):
        z_copy(d, layer).wait_send()

    for j in range(chunks):
        fg_out(j).wait()
    for out in (act_out, bg_out, wg_out):
        out.wait()


def hand_out(*refs):
    sources, results, held = refs[:4], refs[4:8], refs[8:12]
    sem = refs[12]
    loads = [pltpu.make_async_copy(sources[i], held[i], sem.at[0, i]) for i in range(4)]
    stores = [pltpu.make_async_copy(held[i], results[i], sem.at[1, i]) for i in range(4)]
    for load in loads:
        load.start()
    for load, store in zip(loads, stores):
        load.wait()
        store.start()
    for store in stores:
        store.wait()


def solution(mesh):
    n = mesh.shape["rows"]

    def local(features, tiles, columns, live, weight, bias, cotangent):
        nb, slots, tile, _ = tiles.shape
        rows, width = features.shape
        chunk, chunks = tile, nb
        groups = n // PLANE
        part = width // (2 * PLANE)
        vmem, dma = pltpu.VMEM, pltpu.SemaphoreType.DMA
        hbm = pl.BlockSpec(memory_space=pltpu.HBM)
        shapes = (
            jax.ShapeDtypeStruct((rows, width), BF16),
            jax.ShapeDtypeStruct((rows, width), BF16),
            jax.ShapeDtypeStruct((width, width), F32),
            jax.ShapeDtypeStruct((1, width), F32),
        )
        results = pl.pallas_call(
            functools.partial(kernel, n, 1.0 / math.sqrt(rows * n)),
            out_shape=shapes,
            in_specs=[hbm] * 7,
            out_specs=(hbm,) * 4,
            scratch_shapes=[
                vmem((rows, width), BF16),
                vmem((rows, width), BF16),
                vmem((width, width), F32),
                vmem((1, width), F32),
                pltpu.SMEM((nb, slots), jnp.int32),
                pltpu.SMEM((1, nb), jnp.int32),
                vmem((width, width), BF16),
                vmem((1, width), F32),
                vmem((3 * rows, width), BF16),
                vmem((nb + 1, slots, tile, tile), BF16),
                vmem((nb + 1, slots, tile, tile), BF16),
                vmem((rows, 3 * rows), BF16),
                vmem((3 * rows, rows), BF16),
                vmem((rows, width), BF16),
                pltpu.SMEM((nb * slots,), jnp.int32),
                vmem((rows, width), F32),
                vmem((chunks, chunk, width), BF16),
                vmem((chunks, chunk, width), BF16),
                vmem((rows, width), BF16),
                vmem((rows, width), BF16),
                vmem((rows, width), BF16),
                vmem((2, rows, width), BF16),
                vmem((2, rows, width), BF16),
                vmem((chunks, chunk, width), BF16),
                vmem((chunks, chunk, width), BF16),
                vmem((PLANE, part + 16, width), BF16),
                vmem((PLANE, part + 16, width), BF16),
                vmem((groups, part + 16, width), BF16),
                vmem((part, width), BF16),
                vmem((2 * PLANE, part, width), BF16),
                dma((7,)),
                dma((chunks + 3,)),
                dma((chunks + 1,)), dma((chunks + 1,)),
                dma((chunks,)), dma((chunks,)),
                dma((chunks + 1,)), dma((chunks + 1,)),
                dma((chunks,)), dma((chunks,)),
                dma((PLANE - 1,)), dma((PLANE - 1,)),
                dma((groups - 1,)), dma((groups - 1,)),
                dma((2 * PLANE - 1,)), dma((2 * PLANE - 1,)),
            ],
            compiler_params=pltpu.CompilerParams(
                collective_id=0, has_side_effects=True, vmem_limit_bytes=64 * 2**20
            ),
        )(columns, live.T, features, tiles, weight, bias.reshape(1, width), cotangent)
        act, feature_grad, weight_grad, bias_grad = pl.pallas_call(
            hand_out,
            out_shape=shapes,
            in_specs=[hbm] * 4,
            out_specs=(hbm,) * 4,
            scratch_shapes=[vmem(x.shape, x.dtype) for x in shapes] + [dma((2, 4))],
            compiler_params=pltpu.CompilerParams(vmem_limit_bytes=64 * 2**20),
        )(*results)
        return act, feature_grad, weight_grad, bias_grad.reshape(width)

    return jax.shard_map(
        local,
        mesh=mesh,
        in_specs=(
            P("rows", None), P("rows", "rep", None, None), P("rows", "rep"), P("rows", "rep"),
            P(), P(), P("rows", None),
        ),
        out_specs=(P("rows", None), P("rows", None), P(), P()),
        check_vma=False,
    )
```

```python
import functools
import math

import jax
import jax.numpy as jnp
from jax import lax
from jax.experimental import pallas as pl
from jax.experimental.pallas import tpu as pltpu
from jax.sharding import PartitionSpec as P

MESH = pl.DeviceIdType.MESH
PLANE = 4
F32, BF16 = jnp.float32, jnp.bfloat16
NT = (((1,), (1,)), ((), ()))
TN = (((0,), (0,)), ((), ()))


def remote(src, dst, send_sem, recv_sem, device):
    return pltpu.make_async_remote_copy(
        src_ref=src, dst_ref=dst, send_sem=send_sem, recv_sem=recv_sem,
        device_id=device, device_id_type=MESH,
    )


def kernel(
    n, scale,
    cols_hbm, live_hbm, feat_hbm, tiles_hbm, w_hbm, b_hbm, cot_hbm,
    act_hbm, fg_hbm, wg_hbm, bg_hbm,
    act_ref, fg_ref, wg_ref, bg_ref, cols, live, w_ref, b_ref, feat, tiles, band, cot, eff, acc, acc_t,
    p_send, p_recv, agg_all, grad_all, agg_grad_t, s_send, s_recv, t_send, t_recv,
    w_send, w_recv, z_recv, g_send, g_recv,
    local_sem, out_sem, f_ssem, f_rsem, p_ssem, p_rsem, s_ssem, s_rsem, t_ssem, t_rsem,
    w_ssem, w_rsem, z_ssem, z_rsem, g_ssem, g_rsem,
):
    me, rep = lax.axis_index("rows"), lax.axis_index("rep")
    nb, slots, tile = tiles_hbm.shape[0], tiles_hbm.shape[1], tiles_hbm.shape[2]
    rows = nb * tile
    width = w_hbm.shape[0]
    groups = n // PLANE
    quad = lax.rem(me, PLANE)
    layer = lax.div(me, PLANE)
    chunk, chunks = tile, nb
    bulk = 2 * tile
    even = lax.rem(me, 2) == 0
    near = jnp.where(even, me + 1, me - 1)
    far = jnp.where(even, me - 1, me + 1)
    has_far = jnp.logical_and(far >= 0, far < n)
    far_even = jnp.logical_and(has_far, even)
    far_odd = jnp.logical_and(has_far, jnp.logical_not(even))
    partner = (me, 1 - rep)

    def plane_peer(d):
        return lax.rem(quad + d, PLANE)

    def layer_peer(d):
        return lax.rem(layer + d, groups)

    barrier = pltpu.get_barrier_semaphore()

    def greet(device):
        pl.semaphore_signal(barrier, inc=1, device_id=device, device_id_type=MESH)

    @pl.when(has_far)
    def _():
        greet((far, rep))

    greet((near, rep))
    greet(partner)
    for d in range(1, PLANE):
        greet((layer * PLANE + plane_peer(d), rep))
        greet((layer * PLANE + plane_peer(d), 1 - rep))
    for d in range(1, groups):
        greet((layer_peer(d) * PLANE + quad, rep))

    loads = [
        pltpu.make_async_copy(src, dst, local_sem.at[i])
        for i, (src, dst) in enumerate((
            (cols_hbm, cols), (live_hbm, live), (tiles_hbm, tiles.at[pl.ds(0, nb)]),
            (feat_hbm, feat.at[pl.ds(rows, rows)]), (w_hbm, w_ref), (b_hbm, b_ref),
            (cot_hbm, cot),
        ))
    ]
    for load in loads:
        load.start()

    first = (me - 1) * nb
    loads[0].wait()
    loads[1].wait()
    for g in range(nb):
        count = live[0, g]
        for k in range(slots):
            block = cols[g, k] - first
            from_even = jnp.where(block < nb, nb - 1 - block, block)
            from_odd = jnp.where(
                block < nb, block + 2 * nb, jnp.where(block < 2 * nb, block, block - 2 * nb)
            )
            eff[g * slots + k] = jnp.where(
                k < count, jnp.where(even, from_even, from_odd), -1
            )
    loads[3].wait()
    pl.semaphore_wait(barrier, 2 * PLANE - 1 + groups + has_far.astype(jnp.int32))

    def far_feat(j):
        start = pl.multiple_of(jnp.where(even, j, chunks - 1 - j) * chunk, chunk)
        return remote(
            feat.at[pl.ds(rows + start, chunk)], feat.at[pl.ds(j * chunk, chunk)],
            f_ssem.at[j], f_rsem.at[j], (far, rep),
        )

    near_feat = remote(
        feat.at[pl.ds(rows, rows)], feat.at[pl.ds(2 * rows, rows)],
        f_ssem.at[chunks], f_rsem.at[chunks], (near, rep),
    )

    for j in range(chunks):
        @pl.when(has_far if j < chunks - 1 else far_odd)
        def _():
            far_feat(j).start()

    near_feat.start()
    last = (chunks - 1) * chunk

    @pl.when(jnp.logical_not(has_far))
    def _():
        feat[:last] = jnp.zeros((last, width), BF16)
        s_recv[0, :chunks - 1] = jnp.zeros((chunks - 1, width, chunk), BF16)

    @pl.when(jnp.logical_not(far_even))
    def _():
        feat[last:rows] = jnp.zeros((chunk, width), BF16)

    @pl.when(jnp.logical_not(far_odd))
    def _():
        s_recv[0, chunks - 1] = jnp.zeros((width, chunk), BF16)

    tiles[nb, 0] = jnp.zeros((tile, tile), BF16)

    loads[2].wait()

    def slot_of(g, s):
        a, k_at = jnp.int32(nb), jnp.int32(0)
        for k in range(slots):
            hit = eff[g * slots + k] == s
            a = jnp.where(hit, g, a)
            k_at = jnp.where(hit, k, k_at)
        return a, k_at

    def place(s, carry):
        at = pl.ds(pl.multiple_of(s * tile, tile), tile)
        for g in range(nb):
            a, k_at = slot_of(g, s)
            band[g * tile:(g + 1) * tile, at] = tiles[a, k_at]
        return carry

    lax.fori_loop(0, 3 * nb, place, 0)

    def dot(a, b):
        return jnp.dot(a, b, preferred_element_type=F32)

    def chunk_at(m):
        return pl.ds(pl.multiple_of(m * chunk, chunk), chunk)

    def bulk_at(m):
        return pl.ds(pl.multiple_of(m * bulk, bulk), bulk)

    near_feat.wait_recv()

    def near_rows(m, carry):
        acc[bulk_at(m), :] = dot(band[bulk_at(m), rows:], feat[rows:])
        return carry

    lax.fori_loop(0, rows // bulk, near_rows, 0)

    def p_copy(j):
        return remote(p_send.at[j], p_recv.at[j], p_ssem.at[j], p_rsem.at[j], partner)

    def forward_chunk(j):
        return jnp.where(even, chunks - 1 - j, j)

    for j in range(chunks):
        @pl.when(has_far if j < chunks - 1 else far_even)
        def _():
            far_feat(j).wait_recv()

        at, reach = chunk_at(forward_chunk(j)), (j + 1) * chunk
        p_send[j] = (acc[at, :] + dot(band[at, :reach], feat[:reach])).astype(BF16)
        p_copy(j).start()

    for load in loads[4:]:
        load.wait()
    for j in range(chunks):
        at = chunk_at(forward_chunk(j))
        p_copy(j).wait_recv()
        agg = (p_send[j].astype(F32) + p_recv[j].astype(F32)).astype(BF16)
        pre = dot(agg, w_ref[...]) + b_ref[...]
        sig = jax.nn.sigmoid(pre)
        pre_grad = (cot[at, :].astype(F32) * sig * (1.0 + pre * (1.0 - sig))).astype(BF16)
        agg_grad_t[:, at] = lax.dot_general(
            w_ref[...], pre_grad, NT, preferred_element_type=F32
        ).astype(BF16)
        act_ref[at, :] = (pre * sig).astype(BF16)
        agg_all[at, :] = agg
        grad_all[at, :] = pre_grad
    act_out = pltpu.make_async_copy(act_ref, act_hbm, out_sem.at[chunks])
    act_out.start()

    def far_copy(j):
        return remote(
            s_send.at[0, j], s_recv.at[0, j], s_ssem.at[j], s_rsem.at[j], (far, rep)
        )

    near_copy = remote(
        s_send.at[1], s_recv.at[1], s_ssem.at[chunks], s_rsem.at[chunks], (near, rep)
    )

    def far_terms(j):
        at = slice(j * chunk, (j + 1) * chunk)
        s_send[0, j] = dot(agg_grad_t[...], band[:, at]).astype(BF16)

        @pl.when(has_far if j < chunks - 1 else far_even)
        def _():
            far_copy(j).start()

    for j in range(chunks // 2):
        far_terms(j)

    half = width // 2
    part = half // PLANE
    mine = pl.ds(pl.multiple_of(rep * half, half), half)
    w_part = lax.dot_general(agg_all[:, mine], grad_all[...], TN, preferred_element_type=F32)
    b_part = jnp.sum(grad_all[...].astype(F32), axis=0, keepdims=True)
    for c in range(PLANE):
        w_send[c, :part] = w_part[c * part:(c + 1) * part].astype(BF16)
        w_send[c, part:] = jnp.broadcast_to(b_part, (16, width)).astype(BF16)

    def w_copy(d, slot):
        peer = plane_peer(d)
        return remote(
            w_send.at[peer], w_recv.at[slot], w_ssem.at[d - 1], w_rsem.at[d - 1],
            (layer * PLANE + peer, rep),
        )

    for d in range(1, PLANE):
        w_copy(d, quad).start()
    w_recv[quad] = w_send[quad]

    for j in range(chunks // 2, chunks):
        far_terms(j)

    for j in range(0, chunks, 2):
        at = slice(2 * rows + j * chunk, 2 * rows + (j + 2) * chunk)
        terms = dot(agg_grad_t[...], band[:, at]).astype(BF16)
        s_send[1, j] = terms[:, :chunk]
        s_send[1, j + 1] = terms[:, chunk:]
    near_copy.start()

    for j in range(0, chunks, 2):
        at = slice(rows + j * chunk, rows + (j + 2) * chunk)
        terms = dot(agg_grad_t[...], band[:, at])
        acc_t[j] = terms[:, :chunk]
        acc_t[j + 1] = terms[:, chunk:]

    def t_copy(j):
        return remote(t_send.at[j], t_recv.at[j], t_ssem.at[j], t_rsem.at[j], partner)

    def z_copy(d, slot):
        return remote(
            z_recv.at[layer], z_recv.at[slot], z_ssem.at[d - 1], z_rsem.at[d - 1],
            (layer_peer(d) * PLANE + quad, rep),
        )

    def backward_chunk(j):
        return jnp.where(even, j, chunks - 1 - j)

    def g_copy(turn, d, slot):
        at = turn * PLANE + d - 1
        return remote(
            g_send, g_recv.at[slot], g_ssem.at[at], g_rsem.at[at],
            (layer * PLANE + plane_peer(d), 1 - rep if turn else rep),
        )

    others = [(turn, d) for turn in range(2) for d in range(PLANE) if turn or d]

    bg_out = pltpu.make_async_copy(bg_ref, bg_hbm, out_sem.at[chunks + 1])

    def finish_weight():
        for d in range(1, groups):
            z_copy(d, lax.rem(layer + groups - d, groups)).wait_recv()
        total = sum(z_recv[c].astype(F32) for c in range(groups)) * scale
        bg_ref[...] = total[part:part + 1]
        bg_out.start()
        g_send[...] = total[:part].astype(BF16)
        g_recv[rep * PLANE + quad] = total[:part].astype(BF16)

        for turn, d in others:
            g_copy(turn, d, rep * PLANE + quad).start()

    near_copy.wait_recv()
    for j in range(chunks):
        @pl.when(has_far if j < chunks - 1 else far_odd)
        def _():
            far_copy(j).wait_recv()

        m = backward_chunk(j)
        t_send[j] = (
            acc_t[m] + s_recv[0, j].astype(F32) + s_recv[1, m].astype(F32)
        ).astype(BF16)
        t_copy(j).start()
        if j == 1:
            for d in range(1, PLANE):
                w_copy(d, lax.rem(quad + PLANE - d, PLANE)).wait_recv()
            z_recv[layer] = sum(w_recv[c].astype(F32) for c in range(PLANE)).astype(BF16)
            for d in range(1, groups):
                z_copy(d, layer).start()
        if j == chunks - 2:
            finish_weight()

    def fg_out(j):
        at = chunk_at(backward_chunk(j))
        return pltpu.make_async_copy(fg_ref.at[at], fg_hbm.at[at], out_sem.at[j])

    for j in range(chunks):
        t_copy(j).wait_recv()
        fg_ref[chunk_at(backward_chunk(j)), :] = (
            t_send[j].astype(F32) + t_recv[j].astype(F32)
        ).T.astype(BF16)
        fg_out(j).start()

    for turn, d in others:
        source = lax.rem(quad + PLANE - d, PLANE)
        g_copy(turn, d, (1 - rep if turn else rep) * PLANE + source).wait_recv()
    for c in range(2 * PLANE):
        wg_ref[c * part:(c + 1) * part, :] = g_recv[c].astype(F32)
    wg_out = pltpu.make_async_copy(wg_ref, wg_hbm, out_sem.at[chunks + 2])
    wg_out.start()

    for j in range(chunks):
        @pl.when(has_far if j < chunks - 1 else far_odd)
        def _():
            far_feat(j).wait_send()

        @pl.when(has_far if j < chunks - 1 else far_even)
        def _():
            far_copy(j).wait_send()

    near_feat.wait_send()
    near_copy.wait_send()
    for j in range(chunks):
        p_copy(j).wait_send()
        t_copy(j).wait_send()
    for d in range(1, PLANE):
        w_copy(d, quad).wait_send()
    for turn, d in others:
        g_copy(turn, d, rep * PLANE + quad).wait_send()
    for d in range(1, groups):
        z_copy(d, layer).wait_send()

    for j in range(chunks):
        fg_out(j).wait()
    for out in (act_out, bg_out, wg_out):
        out.wait()


def hand_out(*refs):
    sources, results, held = refs[:4], refs[4:8], refs[8:12]
    sem = refs[12]
    loads = [pltpu.make_async_copy(sources[i], held[i], sem.at[0, i]) for i in range(4)]
    stores = [pltpu.make_async_copy(held[i], results[i], sem.at[1, i]) for i in range(4)]
    for load in loads:
        load.start()
    for load, store in zip(loads, stores):
        load.wait()
        store.start()
    for store in stores:
        store.wait()


def solution(mesh):
    n = mesh.shape["rows"]

    def local(features, tiles, columns, live, weight, bias, cotangent):
        nb, slots, tile, _ = tiles.shape
        rows, width = features.shape
        chunk, chunks = tile, nb
        groups = n // PLANE
        part = width // (2 * PLANE)
        vmem, dma = pltpu.VMEM, pltpu.SemaphoreType.DMA
        hbm = pl.BlockSpec(memory_space=pltpu.HBM)
        shapes = (
            jax.ShapeDtypeStruct((rows, width), BF16),
            jax.ShapeDtypeStruct((rows, width), BF16),
            jax.ShapeDtypeStruct((width, width), F32),
            jax.ShapeDtypeStruct((1, width), F32),
        )
        results = pl.pallas_call(
            functools.partial(kernel, n, 1.0 / math.sqrt(rows * n)),
            out_shape=shapes,
            in_specs=[hbm] * 7,
            out_specs=(hbm,) * 4,
            scratch_shapes=[
                vmem((rows, width), BF16),
                vmem((rows, width), BF16),
                vmem((width, width), F32),
                vmem((1, width), F32),
                pltpu.SMEM((nb, slots), jnp.int32),
                pltpu.SMEM((1, nb), jnp.int32),
                vmem((width, width), BF16),
                vmem((1, width), F32),
                vmem((3 * rows, width), BF16),
                vmem((nb + 1, slots, tile, tile), BF16),
                vmem((rows, 3 * rows), BF16),
                vmem((rows, width), BF16),
                pltpu.SMEM((nb * slots,), jnp.int32),
                vmem((rows, width), F32),
                vmem((chunks, width, chunk), F32),
                vmem((chunks, chunk, width), BF16),
                vmem((chunks, chunk, width), BF16),
                vmem((rows, width), BF16),
                vmem((rows, width), BF16),
                vmem((width, rows), BF16),
                vmem((2, chunks, width, chunk), BF16),
                vmem((2, chunks, width, chunk), BF16),
                vmem((chunks, width, chunk), BF16),
                vmem((chunks, width, chunk), BF16),
                vmem((PLANE, part + 16, width), BF16),
                vmem((PLANE, part + 16, width), BF16),
                vmem((groups, part + 16, width), BF16),
                vmem((part, width), BF16),
                vmem((2 * PLANE, part, width), BF16),
                dma((7,)),
                dma((chunks + 3,)),
                dma((chunks + 1,)), dma((chunks + 1,)),
                dma((chunks,)), dma((chunks,)),
                dma((chunks + 1,)), dma((chunks + 1,)),
                dma((chunks,)), dma((chunks,)),
                dma((PLANE - 1,)), dma((PLANE - 1,)),
                dma((groups - 1,)), dma((groups - 1,)),
                dma((2 * PLANE - 1,)), dma((2 * PLANE - 1,)),
            ],
            compiler_params=pltpu.CompilerParams(
                collective_id=0, has_side_effects=True, vmem_limit_bytes=64 * 2**20
            ),
        )(columns, live.T, features, tiles, weight, bias.reshape(1, width), cotangent)
        act, feature_grad, weight_grad, bias_grad = pl.pallas_call(
            hand_out,
            out_shape=shapes,
            in_specs=[hbm] * 4,
            out_specs=(hbm,) * 4,
            scratch_shapes=[vmem(x.shape, x.dtype) for x in shapes] + [dma((2, 4))],
            compiler_params=pltpu.CompilerParams(vmem_limit_bytes=64 * 2**20),
        )(*results)
        return act, feature_grad, weight_grad, bias_grad.reshape(width)

    return jax.shard_map(
        local,
        mesh=mesh,
        in_specs=(
            P("rows", None), P("rows", "rep", None, None), P("rows", "rep"), P("rows", "rep"),
            P(), P(), P("rows", None),
        ),
        out_specs=(P("rows", None), P("rows", None), P(), P()),
        check_vma=False,
    )
```

```python
import functools
import math

import jax
import jax.numpy as jnp
from jax import lax
from jax.experimental import pallas as pl
from jax.experimental.pallas import tpu as pltpu
from jax.sharding import PartitionSpec as P

MESH = pl.DeviceIdType.MESH
PLANE = 4
F32, BF16 = jnp.float32, jnp.bfloat16
NT = (((1,), (1,)), ((), ()))
TN = (((0,), (0,)), ((), ()))


def remote(src, dst, send_sem, recv_sem, device):
    return pltpu.make_async_remote_copy(
        src_ref=src, dst_ref=dst, send_sem=send_sem, recv_sem=recv_sem,
        device_id=device, device_id_type=MESH,
    )


def kernel(
    n, scale,
    cols_hbm, live_hbm, feat_hbm, tiles_hbm, w_hbm, b_hbm, cot_hbm,
    act_hbm, fg_hbm, wg_hbm, bg_hbm,
    act_ref, fg_ref, wg_ref, bg_ref, cols, live, w_ref, b_ref, feat, tiles, band, cot, eff, acc, acc_t,
    p_send, p_recv, agg_all, grad_all, agg_grad_t, s_send, s_recv, t_send, t_recv,
    w_send, w_recv, z_recv, g_send, g_recv,
    local_sem, out_sem, f_ssem, f_rsem, p_ssem, p_rsem, s_ssem, s_rsem, t_ssem, t_rsem,
    w_ssem, w_rsem, z_ssem, z_rsem, g_ssem, g_rsem,
):
    me, rep = lax.axis_index("rows"), lax.axis_index("rep")
    nb, slots, tile = tiles_hbm.shape[0], tiles_hbm.shape[1], tiles_hbm.shape[2]
    rows = nb * tile
    width = w_hbm.shape[0]
    groups = n // PLANE
    quad = lax.rem(me, PLANE)
    layer = lax.div(me, PLANE)
    chunk, chunks = tile, nb
    bulk = 2 * tile
    even = lax.rem(me, 2) == 0
    near = jnp.where(even, me + 1, me - 1)
    far = jnp.where(even, me - 1, me + 1)
    has_far = jnp.logical_and(far >= 0, far < n)
    far_even = jnp.logical_and(has_far, even)
    far_odd = jnp.logical_and(has_far, jnp.logical_not(even))
    partner = (me, 1 - rep)

    def plane_peer(d):
        return lax.rem(quad + d, PLANE)

    def layer_peer(d):
        return lax.rem(layer + d, groups)

    barrier = pltpu.get_barrier_semaphore()

    def greet(device):
        pl.semaphore_signal(barrier, inc=1, device_id=device, device_id_type=MESH)

    @pl.when(has_far)
    def _():
        greet((far, rep))

    greet((near, rep))
    greet(partner)
    for d in range(1, PLANE):
        greet((layer * PLANE + plane_peer(d), rep))
        greet((layer * PLANE + plane_peer(d), 1 - rep))
    for d in range(1, groups):
        greet((layer_peer(d) * PLANE + quad, rep))

    loads = [
        pltpu.make_async_copy(src, dst, local_sem.at[i])
        for i, (src, dst) in enumerate((
            (cols_hbm, cols), (live_hbm, live), (tiles_hbm, tiles.at[pl.ds(0, nb)]),
            (feat_hbm, feat.at[pl.ds(rows, rows)]), (w_hbm, w_ref), (b_hbm, b_ref),
            (cot_hbm, cot),
        ))
    ]
    for load in loads:
        load.start()

    first = (me - 1) * nb
    loads[0].wait()
    loads[1].wait()
    for g in range(nb):
        count = live[0, g]
        for k in range(slots):
            block = cols[g, k] - first
            from_even = jnp.where(block < nb, nb - 1 - block, block)
            from_odd = jnp.where(
                block < nb, block + 2 * nb, jnp.where(block < 2 * nb, block, block - 2 * nb)
            )
            eff[g * slots + k] = jnp.where(
                k < count, jnp.where(even, from_even, from_odd), -1
            )
    loads[3].wait()
    pl.semaphore_wait(barrier, 2 * PLANE - 1 + groups + has_far.astype(jnp.int32))

    def far_feat(j):
        start = pl.multiple_of(jnp.where(even, j, chunks - 1 - j) * chunk, chunk)
        return remote(
            feat.at[pl.ds(rows + start, chunk)], feat.at[pl.ds(j * chunk, chunk)],
            f_ssem.at[j], f_rsem.at[j], (far, rep),
        )

    near_feat = remote(
        feat.at[pl.ds(rows, rows)], feat.at[pl.ds(2 * rows, rows)],
        f_ssem.at[chunks], f_rsem.at[chunks], (near, rep),
    )

    for j in range(chunks):
        @pl.when(has_far if j < chunks - 1 else far_odd)
        def _():
            far_feat(j).start()

    near_feat.start()
    last = (chunks - 1) * chunk

    @pl.when(jnp.logical_not(has_far))
    def _():
        feat[:last] = jnp.zeros((last, width), BF16)
        s_recv[0, :chunks - 1] = jnp.zeros((chunks - 1, width, chunk), BF16)

    @pl.when(jnp.logical_not(far_even))
    def _():
        feat[last:rows] = jnp.zeros((chunk, width), BF16)

    @pl.when(jnp.logical_not(far_odd))
    def _():
        s_recv[0, chunks - 1] = jnp.zeros((width, chunk), BF16)

    tiles[nb, 0] = jnp.zeros((tile, tile), BF16)

    loads[2].wait()

    def slot_of(g, s):
        a, k_at = jnp.int32(nb), jnp.int32(0)
        for k in range(slots):
            hit = eff[g * slots + k] == s
            a = jnp.where(hit, g, a)
            k_at = jnp.where(hit, k, k_at)
        return a, k_at

    def place(s, carry):
        at = pl.ds(pl.multiple_of(s * tile, tile), tile)
        for g in range(nb):
            a, k_at = slot_of(g, s)
            band[g * tile:(g + 1) * tile, at] = tiles[a, k_at]
        return carry

    lax.fori_loop(0, 3 * nb, place, 0)

    def dot(a, b):
        return jnp.dot(a, b, preferred_element_type=F32)

    def chunk_at(m):
        return pl.ds(pl.multiple_of(m * chunk, chunk), chunk)

    def bulk_at(m):
        return pl.ds(pl.multiple_of(m * bulk, bulk), bulk)

    near_feat.wait_recv()

    def near_rows(m, carry):
        acc[bulk_at(m), :] = dot(band[bulk_at(m), rows:], feat[rows:])
        return carry

    lax.fori_loop(0, rows // bulk, near_rows, 0)

    def p_copy(j):
        return remote(p_send.at[j], p_recv.at[j], p_ssem.at[j], p_rsem.at[j], partner)

    def forward_chunk(j):
        return jnp.where(even, chunks - 1 - j, j)

    for j in range(chunks):
        at = chunk_at(forward_chunk(j))

        def add_far(reach):
            p_send[j] = (acc[at, :] + dot(band[at, :reach], feat[:reach])).astype(BF16)

        @pl.when(far_even)
        def _():
            far_feat(j).wait_recv()

        @pl.when(even)
        def _():
            add_far((j + 1) * chunk)

        if j == 0:
            @pl.when(jnp.logical_not(even))
            def _():
                p_send[j] = acc[at, :].astype(BF16)
        else:
            @pl.when(far_odd)
            def _():
                far_feat(j - 1).wait_recv()

            @pl.when(jnp.logical_not(even))
            def _():
                add_far(j * chunk)

        p_copy(j).start()

    for load in loads[4:]:
        load.wait()
    for j in range(chunks):
        at = chunk_at(forward_chunk(j))
        p_copy(j).wait_recv()
        agg = (p_send[j].astype(F32) + p_recv[j].astype(F32)).astype(BF16)
        pre = dot(agg, w_ref[...]) + b_ref[...]
        sig = jax.nn.sigmoid(pre)
        pre_grad = (cot[at, :].astype(F32) * sig * (1.0 + pre * (1.0 - sig))).astype(BF16)
        agg_grad_t[:, at] = lax.dot_general(
            w_ref[...], pre_grad, NT, preferred_element_type=F32
        ).astype(BF16)
        act_ref[at, :] = (pre * sig).astype(BF16)
        agg_all[at, :] = agg
        grad_all[at, :] = pre_grad
    act_out = pltpu.make_async_copy(act_ref, act_hbm, out_sem.at[chunks])
    act_out.start()

    def far_copy(j):
        return remote(
            s_send.at[0, j], s_recv.at[0, j], s_ssem.at[j], s_rsem.at[j], (far, rep)
        )

    near_copy = remote(
        s_send.at[1], s_recv.at[1], s_ssem.at[chunks], s_rsem.at[chunks], (near, rep)
    )

    def far_terms(j):
        at = slice(j * chunk, (j + 1) * chunk)
        s_send[0, j] = dot(agg_grad_t[...], band[:, at]).astype(BF16)

        @pl.when(has_far if j < chunks - 1 else far_even)
        def _():
            far_copy(j).start()

    for j in range(chunks // 2):
        far_terms(j)

    half = width // 2
    part = half // PLANE
    mine = pl.ds(pl.multiple_of(rep * half, half), half)
    w_part = lax.dot_general(agg_all[:, mine], grad_all[...], TN, preferred_element_type=F32)
    b_part = jnp.sum(grad_all[...].astype(F32), axis=0, keepdims=True)
    for c in range(PLANE):
        w_send[c, :part] = w_part[c * part:(c + 1) * part].astype(BF16)
        w_send[c, part:] = jnp.broadcast_to(b_part, (16, width)).astype(BF16)

    def w_copy(d, slot):
        peer = plane_peer(d)
        return remote(
            w_send.at[peer], w_recv.at[slot], w_ssem.at[d - 1], w_rsem.at[d - 1],
            (layer * PLANE + peer, rep),
        )

    for d in range(1, PLANE):
        w_copy(d, quad).start()
    w_recv[quad] = w_send[quad]

    for j in range(chunks // 2, chunks):
        far_terms(j)

    for j in range(0, chunks, 2):
        at = slice(2 * rows + j * chunk, 2 * rows + (j + 2) * chunk)
        terms = dot(agg_grad_t[...], band[:, at]).astype(BF16)
        s_send[1, j] = terms[:, :chunk]
        s_send[1, j + 1] = terms[:, chunk:]
    near_copy.start()

    for j in range(0, chunks, 2):
        at = slice(rows + j * chunk, rows + (j + 2) * chunk)
        terms = dot(agg_grad_t[...], band[:, at])
        acc_t[j] = terms[:, :chunk]
        acc_t[j + 1] = terms[:, chunk:]

    def t_copy(j):
        return remote(t_send.at[j], t_recv.at[j], t_ssem.at[j], t_rsem.at[j], partner)

    def z_copy(d, slot):
        return remote(
            z_recv.at[layer], z_recv.at[slot], z_ssem.at[d - 1], z_rsem.at[d - 1],
            (layer_peer(d) * PLANE + quad, rep),
        )

    def backward_chunk(j):
        return jnp.where(even, j, chunks - 1 - j)

    def g_copy(turn, d, slot):
        at = turn * PLANE + d - 1
        return remote(
            g_send, g_recv.at[slot], g_ssem.at[at], g_rsem.at[at],
            (layer * PLANE + plane_peer(d), 1 - rep if turn else rep),
        )

    others = [(turn, d) for turn in range(2) for d in range(PLANE) if turn or d]

    bg_out = pltpu.make_async_copy(bg_ref, bg_hbm, out_sem.at[chunks + 1])

    def finish_weight():
        for d in range(1, groups):
            z_copy(d, lax.rem(layer + groups - d, groups)).wait_recv()
        total = sum(z_recv[c].astype(F32) for c in range(groups)) * scale
        bg_ref[...] = total[part:part + 1]
        bg_out.start()
        g_send[...] = total[:part].astype(BF16)
        g_recv[rep * PLANE + quad] = total[:part].astype(BF16)

        for turn, d in others:
            g_copy(turn, d, rep * PLANE + quad).start()

    near_copy.wait_recv()
    for j in range(chunks):
        @pl.when(has_far if j < chunks - 1 else far_odd)
        def _():
            far_copy(j).wait_recv()

        m = backward_chunk(j)
        t_send[j] = (
            acc_t[m] + s_recv[0, j].astype(F32) + s_recv[1, m].astype(F32)
        ).astype(BF16)
        t_copy(j).start()
        if j == 2:
            for d in range(1, PLANE):
                w_copy(d, lax.rem(quad + PLANE - d, PLANE)).wait_recv()
            z_recv[layer] = sum(w_recv[c].astype(F32) for c in range(PLANE)).astype(BF16)
            for d in range(1, groups):
                z_copy(d, layer).start()

    finish_weight()

    def fg_out(j):
        at = chunk_at(backward_chunk(j))
        return pltpu.make_async_copy(fg_ref.at[at], fg_hbm.at[at], out_sem.at[j])

    for j in range(chunks):
        t_copy(j).wait_recv()
        fg_ref[chunk_at(backward_chunk(j)), :] = (
            t_send[j].astype(F32) + t_recv[j].astype(F32)
        ).T.astype(BF16)
        fg_out(j).start()

    for turn, d in others:
        source = lax.rem(quad + PLANE - d, PLANE)
        g_copy(turn, d, (1 - rep if turn else rep) * PLANE + source).wait_recv()
    for c in range(2 * PLANE):
        wg_ref[c * part:(c + 1) * part, :] = g_recv[c].astype(F32)
    wg_out = pltpu.make_async_copy(wg_ref, wg_hbm, out_sem.at[chunks + 2])
    wg_out.start()

    for j in range(chunks):
        @pl.when(has_far if j < chunks - 1 else far_odd)
        def _():
            far_feat(j).wait_send()

        @pl.when(has_far if j < chunks - 1 else far_even)
        def _():
            far_copy(j).wait_send()

    near_feat.wait_send()
    near_copy.wait_send()
    for j in range(chunks):
        p_copy(j).wait_send()
        t_copy(j).wait_send()
    for d in range(1, PLANE):
        w_copy(d, quad).wait_send()
    for turn, d in others:
        g_copy(turn, d, rep * PLANE + quad).wait_send()
    for d in range(1, groups):
        z_copy(d, layer).wait_send()

    for j in range(chunks):
        fg_out(j).wait()
    for out in (act_out, bg_out, wg_out):
        out.wait()


def hand_out(*refs):
    sources, results, held = refs[:4], refs[4:8], refs[8:12]
    sem = refs[12]
    loads = [pltpu.make_async_copy(sources[i], held[i], sem.at[0, i]) for i in range(4)]
    stores = [pltpu.make_async_copy(held[i], results[i], sem.at[1, i]) for i in range(4)]
    for load in loads:
        load.start()
    for load, store in zip(loads, stores):
        load.wait()
        store.start()
    for store in stores:
        store.wait()


def solution(mesh):
    n = mesh.shape["rows"]

    def local(features, tiles, columns, live, weight, bias, cotangent):
        nb, slots, tile, _ = tiles.shape
        rows, width = features.shape
        chunk, chunks = tile, nb
        groups = n // PLANE
        part = width // (2 * PLANE)
        vmem, dma = pltpu.VMEM, pltpu.SemaphoreType.DMA
        hbm = pl.BlockSpec(memory_space=pltpu.HBM)
        shapes = (
            jax.ShapeDtypeStruct((rows, width), BF16),
            jax.ShapeDtypeStruct((rows, width), BF16),
            jax.ShapeDtypeStruct((width, width), F32),
            jax.ShapeDtypeStruct((1, width), F32),
        )
        results = pl.pallas_call(
            functools.partial(kernel, n, 1.0 / math.sqrt(rows * n)),
            out_shape=shapes,
            in_specs=[hbm] * 7,
            out_specs=(hbm,) * 4,
            scratch_shapes=[
                vmem((rows, width), BF16),
                vmem((rows, width), BF16),
                vmem((width, width), F32),
                vmem((1, width), F32),
                pltpu.SMEM((nb, slots), jnp.int32),
                pltpu.SMEM((1, nb), jnp.int32),
                vmem((width, width), BF16),
                vmem((1, width), F32),
                vmem((3 * rows, width), BF16),
                vmem((nb + 1, slots, tile, tile), BF16),
                vmem((rows, 3 * rows), BF16),
                vmem((rows, width), BF16),
                pltpu.SMEM((nb * slots,), jnp.int32),
                vmem((rows, width), F32),
                vmem((chunks, width, chunk), F32),
                vmem((chunks, chunk, width), BF16),
                vmem((chunks, chunk, width), BF16),
                vmem((rows, width), BF16),
                vmem((rows, width), BF16),
                vmem((width, rows), BF16),
                vmem((2, chunks, width, chunk), BF16),
                vmem((2, chunks, width, chunk), BF16),
                vmem((chunks, width, chunk), BF16),
                vmem((chunks, width, chunk), BF16),
                vmem((PLANE, part + 16, width), BF16),
                vmem((PLANE, part + 16, width), BF16),
                vmem((groups, part + 16, width), BF16),
                vmem((part, width), BF16),
                vmem((2 * PLANE, part, width), BF16),
                dma((7,)),
                dma((chunks + 3,)),
                dma((chunks + 1,)), dma((chunks + 1,)),
                dma((chunks,)), dma((chunks,)),
                dma((chunks + 1,)), dma((chunks + 1,)),
                dma((chunks,)), dma((chunks,)),
                dma((PLANE - 1,)), dma((PLANE - 1,)),
                dma((groups - 1,)), dma((groups - 1,)),
                dma((2 * PLANE - 1,)), dma((2 * PLANE - 1,)),
            ],
            compiler_params=pltpu.CompilerParams(
                collective_id=0, has_side_effects=True, vmem_limit_bytes=64 * 2**20
            ),
        )(columns, live.T, features, tiles, weight, bias.reshape(1, width), cotangent)
        act, feature_grad, weight_grad, bias_grad = pl.pallas_call(
            hand_out,
            out_shape=shapes,
            in_specs=[hbm] * 4,
            out_specs=(hbm,) * 4,
            scratch_shapes=[vmem(x.shape, x.dtype) for x in shapes] + [dma((2, 4))],
            compiler_params=pltpu.CompilerParams(vmem_limit_bytes=64 * 2**20),
        )(*results)
        return act, feature_grad, weight_grad, bias_grad.reshape(width)

    return jax.shard_map(
        local,
        mesh=mesh,
        in_specs=(
            P("rows", None), P("rows", "rep", None, None), P("rows", "rep"), P("rows", "rep"),
            P(), P(), P("rows", None),
        ),
        out_specs=(P("rows", None), P("rows", None), P(), P()),
        check_vma=False,
    )
```

```python
import functools
import math

import jax
import jax.numpy as jnp
from jax import lax
from jax.experimental import pallas as pl
from jax.experimental.pallas import tpu as pltpu
from jax.sharding import PartitionSpec as P

MESH = pl.DeviceIdType.MESH
PLANE = 4
F32, BF16 = jnp.float32, jnp.bfloat16
NT = (((1,), (1,)), ((), ()))
TN = (((0,), (0,)), ((), ()))


def remote(src, dst, send_sem, recv_sem, device):
    return pltpu.make_async_remote_copy(
        src_ref=src, dst_ref=dst, send_sem=send_sem, recv_sem=recv_sem,
        device_id=device, device_id_type=MESH,
    )


def kernel(
    n, scale,
    cols_hbm, live_hbm, feat_hbm, tiles_hbm, w_hbm, b_hbm, cot_hbm,
    act_hbm, fg_hbm, wg_hbm, bg_hbm,
    act_ref, fg_ref, wg_ref, bg_ref, cols, live, w_ref, b_ref, feat, tiles, band, cot, eff, acc, acc_t,
    p_send, p_recv, agg_all, grad_all, agg_grad_t, s_send, s_recv, t_send, t_recv,
    w_send, w_recv, z_recv, g_send, g_recv,
    local_sem, out_sem, f_ssem, f_rsem, p_ssem, p_rsem, s_ssem, s_rsem, t_ssem, t_rsem,
    w_ssem, w_rsem, z_ssem, z_rsem, g_ssem, g_rsem,
):
    me, rep = lax.axis_index("rows"), lax.axis_index("rep")
    nb, slots, tile = tiles_hbm.shape[0], tiles_hbm.shape[1], tiles_hbm.shape[2]
    rows = nb * tile
    width = w_hbm.shape[0]
    groups = n // PLANE
    quad = lax.rem(me, PLANE)
    layer = lax.div(me, PLANE)
    chunk, chunks = tile, nb
    even = lax.rem(me, 2) == 0
    near = jnp.where(even, me + 1, me - 1)
    far = jnp.where(even, me - 1, me + 1)
    has_far = jnp.logical_and(far >= 0, far < n)
    far_even = jnp.logical_and(has_far, even)
    far_odd = jnp.logical_and(has_far, jnp.logical_not(even))
    partner = (me, 1 - rep)

    def plane_peer(d):
        return lax.rem(quad + d, PLANE)

    def layer_peer(d):
        return lax.rem(layer + d, groups)

    barrier = pltpu.get_barrier_semaphore()

    def greet(device):
        pl.semaphore_signal(barrier, inc=1, device_id=device, device_id_type=MESH)

    @pl.when(has_far)
    def _():
        greet((far, rep))

    greet((near, rep))
    greet(partner)
    for d in range(1, PLANE):
        greet((layer * PLANE + plane_peer(d), rep))
        greet((layer * PLANE + plane_peer(d), 1 - rep))
    for d in range(1, groups):
        greet((layer_peer(d) * PLANE + quad, rep))

    loads = [
        pltpu.make_async_copy(src, dst, local_sem.at[i])
        for i, (src, dst) in enumerate((
            (cols_hbm, cols), (live_hbm, live), (tiles_hbm, tiles.at[pl.ds(0, nb)]),
            (feat_hbm, feat.at[pl.ds(rows, rows)]), (w_hbm, w_ref), (b_hbm, b_ref),
            (cot_hbm, cot),
        ))
    ]
    for load in loads:
        load.start()

    first = (me - 1) * nb
    loads[0].wait()
    loads[1].wait()
    for g in range(nb):
        count = live[0, g]
        for k in range(slots):
            block = cols[g, k] - first
            from_even = jnp.where(block < nb, nb - 1 - block, block)
            from_odd = jnp.where(
                block < nb, block + 2 * nb, jnp.where(block < 2 * nb, block, block - 2 * nb)
            )
            eff[g * slots + k] = jnp.where(
                k < count, jnp.where(even, from_even, from_odd), -1
            )
    loads[3].wait()
    pl.semaphore_wait(barrier, 2 * PLANE - 1 + groups + has_far.astype(jnp.int32))

    def far_feat(j):
        start = pl.multiple_of(jnp.where(even, j, chunks - 1 - j) * chunk, chunk)
        return remote(
            feat.at[pl.ds(rows + start, chunk)], feat.at[pl.ds(j * chunk, chunk)],
            f_ssem.at[j], f_rsem.at[j], (far, rep),
        )

    near_feat = remote(
        feat.at[pl.ds(rows, rows)], feat.at[pl.ds(2 * rows, rows)],
        f_ssem.at[chunks], f_rsem.at[chunks], (near, rep),
    )

    for j in range(chunks):
        @pl.when(has_far if j < chunks - 1 else far_odd)
        def _():
            far_feat(j).start()

    near_feat.start()
    last = (chunks - 1) * chunk

    @pl.when(jnp.logical_not(has_far))
    def _():
        feat[:last] = jnp.zeros((last, width), BF16)
        s_recv[0, :chunks - 1] = jnp.zeros((chunks - 1, width, chunk), BF16)

    @pl.when(jnp.logical_not(far_even))
    def _():
        feat[last:rows] = jnp.zeros((chunk, width), BF16)

    @pl.when(jnp.logical_not(far_odd))
    def _():
        s_recv[0, chunks - 1] = jnp.zeros((width, chunk), BF16)

    tiles[nb, 0] = jnp.zeros((tile, tile), BF16)

    loads[2].wait()

    def slot_of(g, s):
        a, k_at = jnp.int32(nb), jnp.int32(0)
        for k in range(slots):
            hit = eff[g * slots + k] == s
            a = jnp.where(hit, g, a)
            k_at = jnp.where(hit, k, k_at)
        return a, k_at

    def place(s, carry):
        at = pl.ds(pl.multiple_of(s * tile, tile), tile)
        for g in range(nb):
            a, k_at = slot_of(g, s)
            band[g * tile:(g + 1) * tile, at] = tiles[a, k_at]
        return carry

    lax.fori_loop(0, 3 * nb, place, 0)

    def dot(a, b):
        return jnp.dot(a, b, preferred_element_type=F32)

    def chunk_at(m):
        return pl.ds(pl.multiple_of(m * chunk, chunk), chunk)

    near_feat.wait_recv()

    def p_copy(j):
        return remote(p_send.at[j], p_recv.at[j], p_ssem.at[j], p_rsem.at[j], partner)

    def forward_chunk(j):
        return jnp.where(even, chunks - 1 - j, j)

    for j in range(chunks):
        at = chunk_at(forward_chunk(j))
        acc[...] = dot(band[at, rows:], feat[rows:])

        def add_far(reach):
            p_send[j] = (acc[...] + dot(band[at, :reach], feat[:reach])).astype(BF16)

        @pl.when(far_even)
        def _():
            far_feat(j).wait_recv()

        @pl.when(even)
        def _():
            add_far((j + 1) * chunk)

        if j == 0:
            @pl.when(jnp.logical_not(even))
            def _():
                p_send[j] = acc[...].astype(BF16)
        else:
            @pl.when(far_odd)
            def _():
                far_feat(j - 1).wait_recv()

            @pl.when(jnp.logical_not(even))
            def _():
                add_far(j * chunk)

        p_copy(j).start()

    for load in loads[4:]:
        load.wait()
    for j in range(chunks):
        at = chunk_at(forward_chunk(j))
        p_copy(j).wait_recv()
        agg = (p_send[j].astype(F32) + p_recv[j].astype(F32)).astype(BF16)
        pre = dot(agg, w_ref[...]) + b_ref[...]
        sig = jax.nn.sigmoid(pre)
        pre_grad = (cot[at, :].astype(F32) * sig * (1.0 + pre * (1.0 - sig))).astype(BF16)
        agg_grad_t[:, at] = lax.dot_general(
            w_ref[...], pre_grad, NT, preferred_element_type=F32
        ).astype(BF16)
        act_ref[at, :] = (pre * sig).astype(BF16)
        agg_all[at, :] = agg
        grad_all[at, :] = pre_grad
    act_out = pltpu.make_async_copy(act_ref, act_hbm, out_sem.at[chunks])
    act_out.start()

    def far_copy(j):
        return remote(
            s_send.at[0, j], s_recv.at[0, j], s_ssem.at[j], s_rsem.at[j], (far, rep)
        )

    near_copy = remote(
        s_send.at[1], s_recv.at[1], s_ssem.at[chunks], s_rsem.at[chunks], (near, rep)
    )

    def far_terms(j):
        at = slice(j * chunk, (j + 1) * chunk)
        s_send[0, j] = dot(agg_grad_t[...], band[:, at]).astype(BF16)

        @pl.when(has_far if j < chunks - 1 else far_even)
        def _():
            far_copy(j).start()

    for j in range(chunks // 2):
        far_terms(j)

    half = width // 2
    part = half // PLANE
    mine = pl.ds(pl.multiple_of(rep * half, half), half)
    w_part = lax.dot_general(agg_all[:, mine], grad_all[...], TN, preferred_element_type=F32)
    b_part = jnp.sum(grad_all[...].astype(F32), axis=0, keepdims=True)
    for c in range(PLANE):
        w_send[c, :part] = w_part[c * part:(c + 1) * part].astype(BF16)
        w_send[c, part:] = jnp.broadcast_to(b_part, (16, width)).astype(BF16)

    def w_copy(d, slot):
        peer = plane_peer(d)
        return remote(
            w_send.at[peer], w_recv.at[slot], w_ssem.at[d - 1], w_rsem.at[d - 1],
            (layer * PLANE + peer, rep),
        )

    for d in range(1, PLANE):
        w_copy(d, quad).start()
    w_recv[quad] = w_send[quad]

    for j in range(chunks // 2, chunks):
        far_terms(j)

    for j in range(0, chunks, 2):
        at = slice(2 * rows + j * chunk, 2 * rows + (j + 2) * chunk)
        terms = dot(agg_grad_t[...], band[:, at]).astype(BF16)
        s_send[1, j] = terms[:, :chunk]
        s_send[1, j + 1] = terms[:, chunk:]
    near_copy.start()

    for j in range(0, chunks, 2):
        at = slice(rows + j * chunk, rows + (j + 2) * chunk)
        terms = dot(agg_grad_t[...], band[:, at])
        acc_t[j] = terms[:, :chunk]
        acc_t[j + 1] = terms[:, chunk:]

    def t_copy(j):
        return remote(t_send.at[j], t_recv.at[j], t_ssem.at[j], t_rsem.at[j], partner)

    def z_copy(d, slot):
        return remote(
            z_recv.at[layer], z_recv.at[slot], z_ssem.at[d - 1], z_rsem.at[d - 1],
            (layer_peer(d) * PLANE + quad, rep),
        )

    def backward_chunk(j):
        return jnp.where(even, j, chunks - 1 - j)

    def g_copy(turn, d, slot):
        at = turn * PLANE + d - 1
        return remote(
            g_send, g_recv.at[slot], g_ssem.at[at], g_rsem.at[at],
            (layer * PLANE + plane_peer(d), 1 - rep if turn else rep),
        )

    others = [(turn, d) for turn in range(2) for d in range(PLANE) if turn or d]

    bg_out = pltpu.make_async_copy(bg_ref, bg_hbm, out_sem.at[chunks + 1])

    def finish_weight():
        for d in range(1, groups):
            z_copy(d, lax.rem(layer + groups - d, groups)).wait_recv()
        total = sum(z_recv[c].astype(F32) for c in range(groups)) * scale
        bg_ref[...] = total[part:part + 1]
        bg_out.start()
        g_send[...] = total[:part].astype(BF16)
        g_recv[rep * PLANE + quad] = total[:part].astype(BF16)

        for turn, d in others:
            g_copy(turn, d, rep * PLANE + quad).start()

    near_copy.wait_recv()
    for j in range(chunks):
        @pl.when(has_far if j < chunks - 1 else far_odd)
        def _():
            far_copy(j).wait_recv()

        m = backward_chunk(j)
        t_send[j] = (
            acc_t[m] + s_recv[0, j].astype(F32) + s_recv[1, m].astype(F32)
        ).astype(BF16)
        t_copy(j).start()
        if j == 2:
            for d in range(1, PLANE):
                w_copy(d, lax.rem(quad + PLANE - d, PLANE)).wait_recv()
            z_recv[layer] = sum(w_recv[c].astype(F32) for c in range(PLANE)).astype(BF16)
            for d in range(1, groups):
                z_copy(d, layer).start()

    finish_weight()

    def fg_out(j):
        at = chunk_at(backward_chunk(j))
        return pltpu.make_async_copy(fg_ref.at[at], fg_hbm.at[at], out_sem.at[j])

    for j in range(chunks):
        t_copy(j).wait_recv()
        fg_ref[chunk_at(backward_chunk(j)), :] = (
            t_send[j].astype(F32) + t_recv[j].astype(F32)
        ).T.astype(BF16)
        fg_out(j).start()

    for turn, d in others:
        source = lax.rem(quad + PLANE - d, PLANE)
        g_copy(turn, d, (1 - rep if turn else rep) * PLANE + source).wait_recv()
    for c in range(2 * PLANE):
        wg_ref[c * part:(c + 1) * part, :] = g_recv[c].astype(F32)
    wg_out = pltpu.make_async_copy(wg_ref, wg_hbm, out_sem.at[chunks + 2])
    wg_out.start()

    for j in range(chunks):
        @pl.when(has_far if j < chunks - 1 else far_odd)
        def _():
            far_feat(j).wait_send()

        @pl.when(has_far if j < chunks - 1 else far_even)
        def _():
            far_copy(j).wait_send()

    near_feat.wait_send()
    near_copy.wait_send()
    for j in range(chunks):
        p_copy(j).wait_send()
        t_copy(j).wait_send()
    for d in range(1, PLANE):
        w_copy(d, quad).wait_send()
    for turn, d in others:
        g_copy(turn, d, rep * PLANE + quad).wait_send()
    for d in range(1, groups):
        z_copy(d, layer).wait_send()

    for j in range(chunks):
        fg_out(j).wait()
    for out in (act_out, bg_out, wg_out):
        out.wait()


def hand_out(*refs):
    sources, results, held = refs[:4], refs[4:8], refs[8:12]
    sem = refs[12]
    loads = [pltpu.make_async_copy(sources[i], held[i], sem.at[0, i]) for i in range(4)]
    stores = [pltpu.make_async_copy(held[i], results[i], sem.at[1, i]) for i in range(4)]
    for load in loads:
        load.start()
    for load, store in zip(loads, stores):
        load.wait()
        store.start()
    for store in stores:
        store.wait()


def solution(mesh):
    n = mesh.shape["rows"]

    def local(features, tiles, columns, live, weight, bias, cotangent):
        nb, slots, tile, _ = tiles.shape
        rows, width = features.shape
        chunk, chunks = tile, nb
        groups = n // PLANE
        part = width // (2 * PLANE)
        vmem, dma = pltpu.VMEM, pltpu.SemaphoreType.DMA
        hbm = pl.BlockSpec(memory_space=pltpu.HBM)
        shapes = (
            jax.ShapeDtypeStruct((rows, width), BF16),
            jax.ShapeDtypeStruct((rows, width), BF16),
            jax.ShapeDtypeStruct((width, width), F32),
            jax.ShapeDtypeStruct((1, width), F32),
        )
        results = pl.pallas_call(
            functools.partial(kernel, n, 1.0 / math.sqrt(rows * n)),
            out_shape=shapes,
            in_specs=[hbm] * 7,
            out_specs=(hbm,) * 4,
            scratch_shapes=[
                vmem((rows, width), BF16),
                vmem((rows, width), BF16),
                vmem((width, width), F32),
                vmem((1, width), F32),
                pltpu.SMEM((nb, slots), jnp.int32),
                pltpu.SMEM((1, nb), jnp.int32),
                vmem((width, width), BF16),
                vmem((1, width), F32),
                vmem((3 * rows, width), BF16),
                vmem((nb + 1, slots, tile, tile), BF16),
                vmem((rows, 3 * rows), BF16),
                vmem((rows, width), BF16),
                pltpu.SMEM((nb * slots,), jnp.int32),
                vmem((chunk, width), F32),
                vmem((chunks, width, chunk), F32),
                vmem((chunks, chunk, width), BF16),
                vmem((chunks, chunk, width), BF16),
                vmem((rows, width), BF16),
                vmem((rows, width), BF16),
                vmem((width, rows), BF16),
                vmem((2, chunks, width, chunk), BF16),
                vmem((2, chunks, width, chunk), BF16),
                vmem((chunks, width, chunk), BF16),
                vmem((chunks, width, chunk), BF16),
                vmem((PLANE, part + 16, width), BF16),
                vmem((PLANE, part + 16, width), BF16),
                vmem((groups, part + 16, width), BF16),
                vmem((part, width), BF16),
                vmem((2 * PLANE, part, width), BF16),
                dma((7,)),
                dma((chunks + 3,)),
                dma((chunks + 1,)), dma((chunks + 1,)),
                dma((chunks,)), dma((chunks,)),
                dma((chunks + 1,)), dma((chunks + 1,)),
                dma((chunks,)), dma((chunks,)),
                dma((PLANE - 1,)), dma((PLANE - 1,)),
                dma((groups - 1,)), dma((groups - 1,)),
                dma((2 * PLANE - 1,)), dma((2 * PLANE - 1,)),
            ],
            compiler_params=pltpu.CompilerParams(
                collective_id=0, has_side_effects=True, vmem_limit_bytes=64 * 2**20
            ),
        )(columns, live.T, features, tiles, weight, bias.reshape(1, width), cotangent)
        act, feature_grad, weight_grad, bias_grad = pl.pallas_call(
            hand_out,
            out_shape=shapes,
            in_specs=[hbm] * 4,
            out_specs=(hbm,) * 4,
            scratch_shapes=[vmem(x.shape, x.dtype) for x in shapes] + [dma((2, 4))],
            compiler_params=pltpu.CompilerParams(vmem_limit_bytes=64 * 2**20),
        )(*results)
        return act, feature_grad, weight_grad, bias_grad.reshape(width)

    return jax.shard_map(
        local,
        mesh=mesh,
        in_specs=(
            P("rows", None), P("rows", "rep", None, None), P("rows", "rep"), P("rows", "rep"),
            P(), P(), P("rows", None),
        ),
        out_specs=(P("rows", None), P("rows", None), P(), P()),
        check_vma=False,
    )
```
